32 devices in a mesh: dp: 16 (over z, y, x), fsdp: 2 (over core).
Axes of the slice: x: 2, y: 2, z: 4, core: 2. Of those that a mesh axis runs over, the one named last changes fastest.
Arguments:
- tokens: bfloat16 [64, 196, 512], P(('dp', 'fsdp')), may hold values from -6 to 6
- regions: int32 [196], replicated, may hold values from 0 to 3
- rel_index: int32 [2401], replicated, may hold values from 0 to 168
- norm_gains: bfloat16 [2, 2, 512], P(None, None, 'fsdp'), may hold values from 0.5 to 1.5
- norm_shifts: bfloat16 [2, 2, 512], P(None, None, 'fsdp'), may hold values from -1.75 to 1.75
- qkv_weight: bfloat16 [2, 512, 1536], P(None, 'fsdp'), may hold values from -0.25 to 0.25
- qv_bias: bfloat16 [2, 2, 512], P(None, None, 'fsdp'), may hold values from -1.75 to 1.75
- rel_table: bfloat16 [2, 169, 16], P(None, None, 'fsdp'), may hold values from -6 to 6
- proj_weight: bfloat16 [2, 512, 512], P(None, 'fsdp'), may hold values from -0.75 to 0.75
- proj_bias: bfloat16 [2, 512], P(None, 'fsdp'), may hold values from -1.75 to 1.75
- fc1_weight: bfloat16 [2, 512, 2048], P(None, 'fsdp'), may hold values from -0.25 to 0.25
- fc1_bias: bfloat16 [2, 2048], P(None, 'fsdp'), may hold values from -1.75 to 1.75
- fc2_weight: bfloat16 [2, 2048, 512], P(None, 'fsdp'), may hold values from -0.1875 to 0.1875
- fc2_bias: bfloat16 [2, 512], P(None, 'fsdp'), may hold values from -1.75 to 1.75
- cotangent: bfloat16 [64, 196, 512], P(('dp', 'fsdp')), may hold values from -6 to 6
Outputs:
- output: bfloat16 [64, 196, 512], P(('dp', 'fsdp'))
- tokens_grad: float32 [64, 196, 512], P(('dp', 'fsdp'))
- norm_gains_grad: float32 [2, 2, 512], P(None, None, 'fsdp')
- norm_shifts_grad: float32 [2, 2, 512], P(None, None, 'fsdp')
- qkv_weight_grad: float32 [2, 512, 1536], P(None, 'fsdp')
- qv_bias_grad: float32 [2, 2, 512], P(None, None, 'fsdp')
- rel_table_grad: float32 [2, 169, 16], P(None, None, 'fsdp')
- proj_weight_grad: float32 [2, 512, 512], P(None, 'fsdp')
- proj_bias_grad: float32 [2, 512], P(None, 'fsdp')
- fc1_weight_grad: float32 [2, 512, 2048], P(None, 'fsdp')
- fc1_bias_grad: float32 [2, 2048], P(None, 'fsdp')
- fc2_weight_grad: float32 [2, 2048, 512], P(None, 'fsdp')
- fc2_bias_grad: float32 [2, 512], P(None, 'fsdp')
The draws below stay inside these ranges and needn't reach their ends.
All inputs are finite; a program needn't handle non-finite values.
Results may differ from the reference program's by a relative error of at most 0.018.
Values may be sent and summed in bfloat16 or wider, within the bound.
No kernel may reach another device: no remote copies, remote signals or barrier semaphores. Data moves between devices by JAX's collectives and lax.ppermute only.
A program may use at most 192 MiB of HBM per device.

```python
import math
import jax
import jax.numpy as jnp
from jax import lax

D = 512
HEADS = 16
HD = 32
FF = 2048
WIN = 7
IMG = 14
SHIFT = 3
PIX = 196
WT = 49
RELS = 169
IMAGES = 64


def touch_ends(values, rng, smallest, top_value):
    extent = values.shape
    index_at = [jax.random.randint(jax.random.fold_in(rng, axis), (), 0, extent[axis]) for axis in range(len(extent))]
    values = values.at[tuple(index_at)].set(smallest)
    longest = extent.index(max(extent))
    index_at[longest] = (index_at[longest] + 1) % extent[longest]
    return values.at[tuple(index_at)].set(top_value)


def levels(own_key, shape, split, smallest, high):
    loudness = 1.0
    for axis_at, blocks in split:
        heights = jax.random.uniform(jax.random.fold_in(jax.random.fold_in(own_key, 6), axis_at), (blocks,), jnp.float32, smallest / len(split), high / len(split))
        loudness = loudness * jnp.repeat(jnp.exp(heights), shape[axis_at] // blocks).reshape((-1,) + (1,) * (len(shape) - 1 - axis_at))
    return loudness


def scatter_about(key, shape, scale, reach, cuts=(), held_as=jnp.bfloat16):
    gain = levels(key, shape, cuts, -0.22, 0.18) if cuts else 1.0
    entries = jax.random.normal(key, shape, jnp.float32) * scale * gain
    return jnp.minimum(jnp.maximum(entries, -reach), reach).astype(held_as)


def setup_inputs(seed: int = 0) -> dict:
    splits = jax.random.split(jax.random.key(seed), 16)
    return {
        "tokens": scatter_about(splits[0], (IMAGES, PIX, D), 1.0, 6.0, ((0, 32),)),
        "regions": touch_ends(jax.random.randint(splits[1], (PIX,), 0, 4), jax.random.fold_in(splits[1], 1), 0, 3).astype(jnp.int32),
        "rel_index": touch_ends(jax.random.randint(splits[2], (WT * WT,), 0, RELS), jax.random.fold_in(splits[2], 1), 0, RELS - 1).astype(jnp.int32),
        "norm_gains": jnp.clip(1.0 + 0.1 * jax.random.normal(splits[3], (2, 2, D), jnp.float32), 0.5, 1.5).astype(jnp.bfloat16),
        "norm_shifts": scatter_about(splits[4], (2, 2, D), 0.3, 1.75, ((2, 2),)),
        "qkv_weight": scatter_about(splits[5], (2, D, 3 * D), D ** -0.5, 0.25, ((1, 2),)),
        "qv_bias": scatter_about(splits[6], (2, 2, D), 0.3, 1.75, ((2, 2),)),
        "rel_table": scatter_about(splits[7], (2, RELS, HEADS), 1.0, 6.0, ((2, 2),)),
        "proj_weight": scatter_about(splits[8], (2, D, D), (D // 8) ** -0.5, 0.75, ((1, 2),)),
        "proj_bias": scatter_about(splits[9], (2, D), 0.3, 1.75, ((1, 2),)),
        "fc1_weight": scatter_about(splits[10], (2, D, FF), D ** -0.5, 0.25, ((1, 2),)),
        "fc1_bias": scatter_about(splits[11], (2, FF), 0.3, 1.75, ((1, 2),)),
        "fc2_weight": scatter_about(splits[12], (2, FF, D), (FF // 2) ** -0.5, 0.1875, ((1, 2),)),
        "fc2_bias": scatter_about(splits[13], (2, D), 0.3, 1.75, ((1, 2),)),
        "cotangent": scatter_about(splits[14], (IMAGES, PIX, D), 1.0, 6.0, ((0, 32),)),
    }


@jax.custom_vjp
def low(v):
    return lax.optimization_barrier(v.astype(jnp.bfloat16)).astype(jnp.float32)

@jax.custom_vjp
def low_back(v):
    return v

def low_keep(v):
    return (low(v), None)

def low_pass(kept, grad):
    return (grad,)

def back_keep(v):
    return (v, None)

def back_low(kept, grad):
    return (low(grad),)
low.defvjp(low_keep, low_pass)
low_back.defvjp(back_keep, back_low)
norm_eps = 1e-05
highest = lax.Precision.HIGHEST

def layer_norm(values, gain_in, shift_in):
    average = lax.optimization_barrier(jnp.mean(values, -1, keepdims=True))
    centred = values - average
    variance = lax.optimization_barrier(jnp.mean(centred * centred, -1, keepdims=True))
    return centred * lax.rsqrt(variance + norm_eps) * gain_in + shift_in

def to_windows(values, offset):
    images = values.shape[0]
    channels = values.shape[-1]
    across = IMG // WIN
    canvas = values.reshape(images, IMG, IMG, channels)
    if offset:
        canvas = jnp.roll(canvas, (-offset, -offset), axis=(1, 2))
    canvas = canvas.reshape(images, across, WIN, across, WIN, channels).transpose(0, 1, 3, 2, 4, 5)
    return canvas.reshape(images * across * across, WIN * WIN, channels)

def from_windows(windows, images, offset):
    channels = windows.shape[-1]
    across = IMG // WIN
    canvas = windows.reshape(images, across, across, WIN, WIN, channels).transpose(0, 1, 3, 2, 4, 5)
    canvas = canvas.reshape(images, IMG, IMG, channels)
    if offset:
        canvas = jnp.roll(canvas, (offset, offset), axis=(1, 2))
    return canvas.reshape(images, IMG * IMG, channels)

def block(tokens_in, params, offset, region_mask, rel_index):
    gains, shifts_in, qkv_w, qv_b, table, proj_w, proj_b, up_w, up_b, down_w, down_b = params
    images = tokens_in.shape[0]
    normed = low(layer_norm(tokens_in, gains[0], shifts_in[0]))
    windows = to_windows(normed, offset)
    count = windows.shape[0]
    projected = jnp.einsum('wtd,de->wte', windows, qkv_w, precision=highest)
    queries = low_back(low(projected[..., :D] + qv_b[0])).reshape(count, WT, HEADS, HD)
    keys_all = low_back(low(projected[..., D:2 * D])).reshape(count, WT, HEADS, HD)
    values_all = low_back(low(projected[..., 2 * D:] + qv_b[1])).reshape(count, WT, HEADS, HD)
    position_bias = table[rel_index].T.reshape(HEADS, WT, WT)
    scores = HD ** (-0.5) * jnp.einsum('wqhc,wkhc->whqk', queries, keys_all, precision=highest) + position_bias[None]
    if region_mask is not None:
        scores = scores + jnp.tile(region_mask, (images, 1, 1))[:, None]
    scores = low_back(scores)
    largest = lax.optimization_barrier(jnp.max(scores, -1, keepdims=True))
    expo = jnp.exp(scores - largest)
    probs = low(expo / lax.optimization_barrier(jnp.sum(expo, -1, keepdims=True)))
    attended = jnp.einsum('whqk,wkhc->wqhc', probs, values_all, precision=highest)
    attended = low_back(low(attended)).reshape(count, WT, D)
    branch = low_back(jnp.einsum('wtd,de->wte', attended, proj_w, precision=highest) + proj_b)
    middle = tokens_in + from_windows(branch, images, offset)
    normed_two = low(layer_norm(middle, gains[1], shifts_in[1]))
    hidden_pre = low_back(jnp.einsum('ntd,df->ntf', normed_two, up_w, precision=highest) + up_b)
    hidden = low(jax.nn.gelu(hidden_pre, approximate=False))
    mlp_out = low_back(jnp.einsum('ntf,fd->ntd', hidden, down_w, precision=highest) + down_b)
    return middle + mlp_out

def reference(tokens, regions, rel_index, norm_gains, norm_shifts, qkv_weight, qv_bias, rel_table, proj_weight, proj_bias, fc1_weight, fc1_bias, fc2_weight, fc2_bias, cotangent):
    params = tuple((item.astype(jnp.float32) for item in (norm_gains, norm_shifts, qkv_weight, qv_bias, rel_table, proj_weight, proj_bias, fc1_weight, fc1_bias, fc2_weight, fc2_bias)))
    region_win = to_windows(regions.reshape(1, PIX, 1), 0).reshape(-1, WT)
    region_mask = jnp.where(region_win[:, :, None] == region_win[:, None, :], 0.0, -100.0).astype(jnp.float32)
    group_size = math.gcd(IMAGES, 16)
    group_count = IMAGES // group_size

    def forward(weights, inputs):

        def one_group(group_in):
            current = group_in
            for layer_at in range(2):
                chosen = tuple((item[layer_at] for item in weights))
                current = block(current, chosen, layer_at * SHIFT, region_mask if layer_at else None, rel_index)
            return current
        stacked = inputs.reshape(group_count, group_size, PIX, D)
        return lax.map(jax.checkpoint(one_group), stacked).reshape(IMAGES, PIX, D)
    result, pull = jax.vjp(forward, params, tokens.astype(jnp.float32))
    grads, tokens_grad = pull(cotangent.astype(jnp.float32))
    return (result.astype(jnp.bfloat16), tokens_grad, grads[0], grads[1], grads[2], grads[3], grads[4], grads[5], grads[6], grads[7], grads[8], grads[9], grads[10])
```

```python
import jax
import jax.numpy as jnp
from jax import lax
from jax.sharding import PartitionSpec as P

D = 512
HEADS = 16
HD = 32
WIN = 7
IMG = 14
SHIFT = 3
PIX = 196
WT = 49
RELS = 169


norm_eps = 1e-05
highest = lax.Precision.HIGHEST


def layer_norm(values, gain_in, shift_in):
    average = jnp.mean(values, -1, keepdims=True)
    centred = values - average
    variance = jnp.mean(centred * centred, -1, keepdims=True)
    return centred * lax.rsqrt(variance + norm_eps) * gain_in + shift_in


def to_windows(values, offset):
    images = values.shape[0]
    channels = values.shape[-1]
    across = IMG // WIN
    canvas = values.reshape(images, IMG, IMG, channels)
    if offset:
        canvas = jnp.roll(canvas, (-offset, -offset), axis=(1, 2))
    canvas = canvas.reshape(images, across, WIN, across, WIN, channels).transpose(0, 1, 3, 2, 4, 5)
    return canvas.reshape(images * across * across, WIN * WIN, channels)


def from_windows(windows, images, offset):
    channels = windows.shape[-1]
    across = IMG // WIN
    canvas = windows.reshape(images, across, across, WIN, WIN, channels).transpose(0, 1, 3, 2, 4, 5)
    canvas = canvas.reshape(images, IMG, IMG, channels)
    if offset:
        canvas = jnp.roll(canvas, (offset, offset), axis=(1, 2))
    return canvas.reshape(images, IMG * IMG, channels)


def split_heads(rows_in):
    return rows_in.reshape(-1, WT, HEADS, HD)


def attend_probs(queries, keys_all, table, region_mask, onehot_low):
    bias_rows = jnp.dot(onehot_low, table, preferred_element_type=jnp.float32)
    position_bias = bias_rows.T.reshape(HEADS, WT, WT)
    scores = (
        HD ** (-0.5)
        * jnp.einsum("wqhc,wkhc->whqk", queries, keys_all, preferred_element_type=jnp.float32)
        + position_bias[None]
    )
    if region_mask is not None:
        scores = scores + region_mask[:, None]
    largest = jnp.max(scores, -1, keepdims=True)
    expo = jnp.exp(scores - largest)
    return expo / jnp.sum(expo, -1, keepdims=True)


def exact_gelu(inner):
    return jax.nn.gelu(inner, approximate=False)


def layer_forward(tokens_in, params, offset, region_mask, onehot_low):
    gains, shifts_in, qkv_w, qv_b, table, proj_w, proj_b, up_w, up_b, down_w, down_b = params
    images = tokens_in.shape[0]
    gain_f = gains.astype(jnp.float32)
    shift_f = shifts_in.astype(jnp.float32)
    normed = layer_norm(tokens_in, gain_f[0], shift_f[0]).astype(jnp.bfloat16)
    windows = to_windows(normed, offset).reshape(-1, D)
    projected = jnp.dot(windows, qkv_w, preferred_element_type=jnp.float32)
    bias_f = qv_b.astype(jnp.float32)
    queries = split_heads((projected[:, :D] + bias_f[0]).astype(jnp.bfloat16))
    keys_all = split_heads(projected[:, D : 2 * D].astype(jnp.bfloat16))
    values_all = split_heads((projected[:, 2 * D :] + bias_f[1]).astype(jnp.bfloat16))
    probs = attend_probs(queries, keys_all, table, region_mask, onehot_low)
    attended = jnp.einsum(
        "whqk,wkhc->wqhc",
        probs.astype(jnp.bfloat16),
        values_all,
        preferred_element_type=jnp.float32,
    )
    attended = attended.astype(jnp.bfloat16).reshape(-1, D)
    branch = jnp.dot(attended, proj_w, preferred_element_type=jnp.float32) + proj_b.astype(
        jnp.float32
    )
    middle = tokens_in + from_windows(branch.reshape(-1, WT, D), images, offset)
    normed_two = layer_norm(middle, gain_f[1], shift_f[1]).astype(jnp.bfloat16).reshape(-1, D)
    hidden_pre = jnp.dot(normed_two, up_w, preferred_element_type=jnp.float32) + up_b.astype(
        jnp.float32
    )
    hidden = exact_gelu(hidden_pre).astype(jnp.bfloat16)
    mlp_out = jnp.dot(hidden, down_w, preferred_element_type=jnp.float32) + down_b.astype(
        jnp.float32
    )
    result = middle + mlp_out.reshape(middle.shape)
    return (
        result,
        (
            tokens_in,
            windows,
            queries,
            keys_all,
            values_all,
            attended,
            middle,
            normed_two,
            hidden_pre,
            hidden,
        ),
    )


def layer_backward(grad_out, saved, params, offset, region_mask, onehot_low, onehot_full):
    gains, shifts_in, qkv_w, qv_b, table, proj_w, proj_b, up_w, up_b, down_w, down_b = params
    (
        tokens_in,
        windows,
        queries,
        keys_all,
        values_all,
        attended,
        middle,
        normed_two,
        hidden_pre,
        hidden,
    ) = saved
    images = tokens_in.shape[0]
    gain_f = gains.astype(jnp.float32)
    shift_f = shifts_in.astype(jnp.float32)
    mlp_grad = grad_out.reshape(-1, D).astype(jnp.bfloat16)
    down_b_grad = jnp.sum(mlp_grad.astype(jnp.float32), 0)
    hidden_grad = jnp.einsum("nd,fd->nf", mlp_grad, down_w, preferred_element_type=jnp.float32)
    gelu_out, gelu_pull = jax.vjp(exact_gelu, hidden_pre)
    pre_grad = gelu_pull(hidden_grad)[0].astype(jnp.bfloat16)
    up_b_grad = jnp.sum(pre_grad.astype(jnp.float32), 0)
    normed_two_grad = jnp.einsum("nf,df->nd", pre_grad, up_w, preferred_element_type=jnp.float32)
    norm_out, norm_pull = jax.vjp(layer_norm, middle, gain_f[1], shift_f[1])
    middle_part, gain_two_grad, shift_two_grad = norm_pull(normed_two_grad.reshape(middle.shape))
    middle_grad = grad_out + middle_part
    branch_grad = to_windows(middle_grad, offset).reshape(-1, D).astype(jnp.bfloat16)
    proj_b_grad = jnp.sum(branch_grad.astype(jnp.float32), 0)
    attended_grad = jnp.einsum("ne,de->nd", branch_grad, proj_w, preferred_element_type=jnp.float32)
    attended_grad = split_heads(attended_grad.astype(jnp.bfloat16))
    probs = attend_probs(queries, keys_all, table, region_mask, onehot_low)
    probs_grad = jnp.einsum(
        "wqhc,wkhc->whqk", attended_grad, values_all, preferred_element_type=jnp.float32
    )
    values_grad = jnp.einsum(
        "whqk,wqhc->wkhc",
        probs.astype(jnp.bfloat16),
        attended_grad,
        preferred_element_type=jnp.float32,
    ).astype(jnp.bfloat16)
    row_delta = jnp.sum(probs_grad * probs, -1, keepdims=True)
    scores_grad = (probs * (probs_grad - row_delta)).astype(jnp.bfloat16)
    head_scale = HD ** (-0.5)
    queries_grad = (
        head_scale
        * jnp.einsum("whqk,wkhc->wqhc", scores_grad, keys_all, preferred_element_type=jnp.float32)
    ).astype(jnp.bfloat16)
    keys_grad = (
        head_scale
        * jnp.einsum("whqk,wqhc->wkhc", scores_grad, queries, preferred_element_type=jnp.float32)
    ).astype(jnp.bfloat16)
    pair_grad = jnp.sum(scores_grad.astype(jnp.float32), 0).reshape(HEADS, WT * WT)
    table_grad = jnp.dot(pair_grad, onehot_full, precision=highest).T
    queries_flat = queries_grad.reshape(-1, D)
    values_flat = values_grad.reshape(-1, D)
    joined_grad = jnp.concatenate([queries_flat, keys_grad.reshape(-1, D), values_flat], axis=1)
    qv_b_grad = jnp.stack(
        [jnp.sum(queries_flat.astype(jnp.float32), 0), jnp.sum(values_flat.astype(jnp.float32), 0)]
    )
    normed_grad = jnp.einsum("ne,de->nd", joined_grad, qkv_w, preferred_element_type=jnp.float32)
    normed_grad = from_windows(normed_grad.reshape(-1, WT, D), images, offset)
    first_out, first_pull = jax.vjp(layer_norm, tokens_in, gain_f[0], shift_f[0])
    input_part, gain_one_grad, shift_one_grad = first_pull(normed_grad)
    input_grad = middle_grad + input_part
    small = [
        jnp.stack([gain_one_grad, gain_two_grad]),
        jnp.stack([shift_one_grad, shift_two_grad]),
        qv_b_grad,
        table_grad,
        proj_b_grad,
        up_b_grad,
        down_b_grad,
    ]
    factors = [
        (windows, joined_grad),
        (attended, branch_grad),
        (normed_two, pre_grad),
        (hidden, mlp_grad),
    ]
    return (input_grad, small, factors)


def swap_cores(value):
    return lax.ppermute(value, "fsdp", [(0, 1), (1, 0)])


def gather_cores(own, axis):
    other = swap_cores(own)
    first = lax.axis_index("fsdp") == 0
    return jnp.concatenate([jnp.where(first, own, other), jnp.where(first, other, own)], axis=axis)


def add_low(one, two):
    return (one.astype(jnp.float32) + two.astype(jnp.float32)).astype(jnp.bfloat16)


def dp_bit(bit):
    return (lax.axis_index("dp") >> bit) & 1


def dp_swap(value, bit, count):
    return lax.ppermute(value, "dp", [(at, at ^ (1 << bit)) for at in range(count)])


def halve(value, bit, count):
    half = value.shape[0] // 2
    side = dp_bit(bit)
    keep = lax.dynamic_slice_in_dim(value, side * half, half, 0)
    send = lax.dynamic_slice_in_dim(value, (1 - side) * half, half, 0)
    return add_low(keep, dp_swap(send, bit, count))


def unhalve(value, bit, count):
    other = dp_swap(value, bit, count)
    first = dp_bit(bit) == 0
    return jnp.concatenate([jnp.where(first, value, other), jnp.where(first, other, value)], axis=0)


def dp_reduce(bucket, count):
    bits = count.bit_length() - 1
    half = bucket.shape[0] // 2
    done = []
    for piece, order in ((bucket[:half], (0, 1)), (bucket[half:], (1, 0))):
        for bit in order:
            piece = halve(piece, bit, count)
        for bit in range(2, bits):
            piece = add_low(piece, dp_swap(piece, bit, count))
        for bit in order[::-1]:
            piece = unhalve(piece, bit, count)
        done.append(piece)
    return jnp.concatenate(done, axis=0)


def columns_to_rows(value):
    return jnp.concatenate([value[:, at : at + D] for at in range(0, value.shape[1], D)], axis=0)


def rows_to_columns(value, rows):
    return jnp.concatenate([value[at : at + rows] for at in range(0, value.shape[0], rows)], axis=1)


def core_split(matrix):
    half = matrix.shape[0] // 2
    core = lax.axis_index("fsdp")
    low = matrix.astype(jnp.bfloat16)
    keep = lax.dynamic_slice_in_dim(low, core * half, half, 0)
    send = lax.dynamic_slice_in_dim(low, (1 - core) * half, half, 0)
    return columns_to_rows(keep), columns_to_rows(send)


def body(
    tokens,
    regions,
    rel_index,
    norm_gains,
    norm_shifts,
    qkv_weight,
    qv_bias,
    rel_table,
    proj_weight,
    proj_bias,
    fc1_weight,
    fc1_bias,
    fc2_weight,
    fc2_bias,
    cotangent,
):
    count = lax.axis_size("dp")
    whole = (
        gather_cores(norm_gains, 2),
        gather_cores(norm_shifts, 2),
        gather_cores(qkv_weight, 1),
        gather_cores(qv_bias, 2),
        gather_cores(rel_table, 2),
        gather_cores(proj_weight, 1),
        gather_cores(proj_bias, 1),
        gather_cores(fc1_weight, 1),
        gather_cores(fc1_bias, 1),
        gather_cores(fc2_weight, 1),
        gather_cores(fc2_bias, 1),
    )
    offsets_all = jnp.arange(RELS, dtype=jnp.int32)
    onehot_full = (rel_index[:, None] == offsets_all[None, :]).astype(jnp.float32)
    onehot_low = onehot_full.astype(jnp.bfloat16)
    region_win = to_windows(regions.reshape(1, PIX, 1), 0).reshape(-1, WT)
    region_base = jnp.where(region_win[:, :, None] == region_win[:, None, :], 0.0, -100.0).astype(
        jnp.float32
    )
    region_mask = jnp.tile(region_base, (tokens.shape[0], 1, 1))
    current = tokens.astype(jnp.float32)
    saved_all = []
    params_all = [tuple(item[layer_at] for item in whole) for layer_at in range(2)]
    for layer_at in range(2):
        current, saved = layer_forward(
            current,
            params_all[layer_at],
            layer_at * SHIFT,
            region_mask if layer_at else None,
            onehot_low,
        )
        saved_all.append(saved)
    output = current.astype(jnp.bfloat16)
    grad_now = cotangent.astype(jnp.float32)
    weight_sums = [None, None]
    smalls = [None, None]
    for layer_at in (1, 0):
        grad_now, small, factors = layer_backward(
            grad_now,
            saved_all[layer_at],
            params_all[layer_at],
            layer_at * SHIFT,
            region_mask if layer_at else None,
            onehot_low,
            onehot_full,
        )
        smalls[layer_at] = small
        pairs = [
            core_split(jnp.einsum("na,nb->ab", left, right, preferred_element_type=jnp.float32))
            for left, right in factors
        ]
        buckets = []
        for chosen in ((2, 3), (0, 1)):
            keep = jnp.concatenate([pairs[at][0] for at in chosen], axis=0)
            send = jnp.concatenate([pairs[at][1] for at in chosen], axis=0)
            buckets.append(dp_reduce(add_low(keep, swap_cores(send)), count))
        weight_sums[layer_at] = buckets
    packed = []
    for layer_at in range(2):
        for item in smalls[layer_at]:
            flat = item.reshape(-1)
            flat = jnp.pad(flat, (0, -flat.size % D))
            packed.append(flat.reshape(-1, D))
    packed = jnp.concatenate(packed, axis=0)
    rows = packed.shape[0]
    packed = jnp.pad(packed, ((0, -rows % 128), (0, 0))).astype(jnp.bfloat16)
    packed = dp_reduce(add_low(packed, swap_cores(packed)), count).astype(jnp.float32)
    core = lax.axis_index("fsdp")
    at = 0
    small_out = [[], []]
    for layer_at in range(2):
        for item in smalls[layer_at]:
            used = -(-item.size // D)
            flat = packed[at : at + used].reshape(-1)[: item.size]
            at += used
            full = flat.reshape(item.shape)
            half = item.shape[-1] // 2
            small_out[layer_at].append(
                lax.dynamic_slice_in_dim(full, core * half, half, full.ndim - 1)
            )
    gains_g, shifts_g, qv_g, table_g, proj_b_g, up_b_g, down_b_g = [
        jnp.stack([small_out[0][at], small_out[1][at]]) for at in range(7)
    ]
    big = [[], [], [], []]
    for layer_at in range(2):
        mlp, attn = weight_sums[layer_at]
        rows = D // 2
        big[0].append(rows_to_columns(attn[: 3 * rows], rows))
        big[1].append(attn[3 * rows :])
        big[2].append(rows_to_columns(mlp[: 4 * rows], rows))
        big[3].append(mlp[4 * rows :])
    qkv_g, proj_g, up_g, down_g = [jnp.stack(item).astype(jnp.float32) for item in big]
    return (
        output,
        grad_now,
        gains_g,
        shifts_g,
        qkv_g,
        qv_g,
        table_g,
        proj_g,
        proj_b_g,
        up_g,
        up_b_g,
        down_g,
        down_b_g,
    )


def solution(mesh):
    return jax.shard_map(
        body,
        mesh=mesh,
        in_specs=(
            P(("dp", "fsdp"), None, None),
            P(),
            P(),
            P(None, None, "fsdp"),
            P(None, None, "fsdp"),
            P(None, "fsdp", None),
            P(None, None, "fsdp"),
            P(None, None, "fsdp"),
            P(None, "fsdp", None),
            P(None, "fsdp"),
            P(None, "fsdp", None),
            P(None, "fsdp"),
            P(None, "fsdp", None),
            P(None, "fsdp"),
            P(("dp", "fsdp"), None, None),
        ),
        out_specs=(
            P(("dp", "fsdp"), None, None),
            P(("dp", "fsdp"), None, None),
            P(None, None, "fsdp"),
            P(None, None, "fsdp"),
            P(None, "fsdp", None),
            P(None, None, "fsdp"),
            P(None, None, "fsdp"),
            P(None, "fsdp", None),
            P(None, "fsdp"),
            P(None, "fsdp", None),
            P(None, "fsdp"),
            P(None, "fsdp", None),
            P(None, "fsdp"),
        ),
        check_vma=False,
    )
```

```python
import functools

import numpy as np

import jax
import jax.numpy as jnp
from jax import lax
from jax.experimental import pallas as pl
from jax.experimental.pallas import tpu as pltpu
from jax.sharding import PartitionSpec as P

D = 512
HEADS = 16
HD = 32
FF = 2048
WIN = 7
IMG = 14
SHIFT = 3
PIX = 196
WT = 49
RELS = 169
ROWS = 64
CELL = 256
QUADS = 4
LIVE = 176

norm_eps = 1e-05
scale = HD**-0.5
f32 = jnp.float32
bf16 = jnp.bfloat16


def place(offset):
    rows = np.full((CELL,), -1, np.int64)
    for i in range(IMG):
        for j in range(IMG):
            window = (i // WIN) * 2 + j // WIN
            row = window * ROWS + (i % WIN) * WIN + j % WIN
            rows[row] = ((i + offset) % IMG) * IMG + (j + offset) % IMG
    return rows


def permutations():
    base, moved = place(0), place(SHIFT)
    lay = np.zeros((CELL, PIX), np.float32)
    lay[base >= 0, base[base >= 0]] = 1
    shifted = np.zeros((CELL, PIX), np.float32)
    shifted[moved >= 0, moved[moved >= 0]] = 1
    return lay, lay.T.copy(), shifted @ lay.T, lay @ shifted.T


def dot(a, b):
    return jnp.dot(a, b, preferred_element_type=f32)


def dot_nt(a, b):
    return lax.dot_general(a, b, (((1,), (1,)), ((), ())), preferred_element_type=f32)


def dot_tn(a, b):
    return lax.dot_general(a, b, (((0,), (0,)), ((), ())), preferred_element_type=f32)


def loop(count, step):
    def run(at, carry):
        step(at)
        return carry

    lax.fori_loop(0, count, run, 0)


def span(at, size):
    return pl.ds(pl.multiple_of(at * size, size), size)


def normal(values):
    centred = values - jnp.mean(values, -1, keepdims=True)
    spread = lax.rsqrt(jnp.mean(centred * centred, -1, keepdims=True) + norm_eps)
    return centred * spread, spread


def norm_rows(source, target, gain, shift, rows):
    def step(at):
        part = span(at, 128)
        unit, _ = normal(source[part, :])
        target[part, :] = (unit * gain + shift).astype(bf16)

    loop(rows // 128, step)


def norm_back(grad, source, gain, extra, target, rows):
    def step(at, sums):
        part = span(at, 128)
        dh = grad[part, :]
        unit, spread = normal(source[part, :])
        du = dh * gain
        back = spread * (
            du
            - jnp.mean(du, -1, keepdims=True)
            - unit * jnp.mean(du * unit, -1, keepdims=True)
        )
        target[part, :] = extra[part, :] + back
        return (
            sums[0] + jnp.sum(dh * unit, 0, keepdims=True),
            sums[1] + jnp.sum(dh, 0, keepdims=True),
        )

    zero = jnp.zeros((1, D), f32)
    return lax.fori_loop(0, rows // 128, step, (zero, zero))


def move(matrix, source, target, rows, columns):
    for image in range(rows // CELL):
        for at in range(columns // D):
            target[image * CELL : (image + 1) * CELL, at * D : (at + 1) * D] = dot(
                matrix, source[image * CELL : (image + 1) * CELL, at * D : (at + 1) * D]
            ).astype(bf16)


def fetch(core, layer, own, other, target, sems):
    half = own.shape[1]
    mine = pltpu.make_async_copy(
        own.at[layer], target.at[pl.ds(pl.multiple_of(core * half, half), half), :], sems.at[0]
    )
    theirs = pltpu.make_async_copy(
        other.at[layer],
        target.at[pl.ds(pl.multiple_of((1 - core) * half, half), half), :],
        sems.at[1],
    )
    mine.start()
    theirs.start()

    def wait():
        mine.wait()
        theirs.wait()

    return wait


def give(core, grads, keep, send, sems):
    one = pltpu.make_async_copy(grads.at[core], keep, sems.at[0])
    two = pltpu.make_async_copy(grads.at[1 - core], send, sems.at[1])
    one.start()
    two.start()
    one.wait()
    two.wait()


def head_masks():
    lanes = lax.broadcasted_iota(jnp.int32, (ROWS, 128), 1) // HD
    return [lanes == at for at in range(QUADS)]


def stack_heads(value, masks):
    zero = jnp.zeros_like(value)
    return jnp.concatenate([jnp.where(mask, value, zero) for mask in masks], axis=0)


def pick_heads(value, masks):
    result = value[:ROWS]
    for at in range(1, QUADS):
        result = jnp.where(masks[at], value[at * ROWS : (at + 1) * ROWS], result)
    return result


def attention_forward_kernel(
    layer,
    rows,
    core_ref,
    source,
    lay,
    to_moved,
    from_moved,
    small,
    bias,
    mask,
    qkv_own,
    qkv_other,
    proj_own,
    proj_other,
    middle,
    normed,
    qkv,
    probs,
    mixed,
    qkv_w,
    proj_w,
    tokens_in,
    work,
    sems,
):
    core = core_ref[0]
    wait_qkv = fetch(core, layer, qkv_own, qkv_other, qkv_w, sems.at[0])
    wait_proj = fetch(core, layer, proj_own, proj_other, proj_w, sems.at[1])
    if layer == 0:
        for image in range(rows // CELL):
            tokens_in[image * CELL : (image + 1) * CELL, :] = dot(lay[...], source[image])
    else:
        tokens_in = source
    norm_rows(tokens_in, normed, small[0:1, :], small[2:3, :], rows)
    if layer == 0:
        moved = normed
    else:
        move(to_moved[...], normed, work, rows, D)
        moved = work
    wait_qkv()
    for at in range(3):
        part = dot(moved[...], qkv_w[:, at * D : (at + 1) * D])
        if at == 0:
            part = part + small[4:5, :]
        if at == 2:
            part = part + small[5:6, :]
        qkv[:, at * D : (at + 1) * D] = part.astype(bf16)
    masks = head_masks()
    out = mixed if layer == 0 else work

    def window(at):
        part = span(at, ROWS)
        for quad in range(QUADS):
            lanes = slice(quad * 128, (quad + 1) * 128)
            queries = stack_heads(qkv[part, lanes], masks)
            keys = qkv[part, D + quad * 128 : D + (quad + 1) * 128]
            values = qkv[part, 2 * D + quad * 128 : 2 * D + (quad + 1) * 128]
            scores = scale * dot_nt(keys, queries) + bias[quad]
            if layer:
                scores = scores + mask[at % 4]
            expo = jnp.exp(scores - jnp.max(scores, 0, keepdims=True))
            prob = expo / jnp.sum(expo, 0, keepdims=True)
            probs[at, quad] = prob
            mix = dot_tn(prob.astype(bf16), values)
            out[part, lanes] = pick_heads(mix, masks).astype(bf16)

    loop(rows // ROWS, window)
    if layer:
        move(from_moved[...], work, mixed, rows, D)
    wait_proj()
    middle[...] = tokens_in[...] + dot(mixed[...], proj_w[...]) + small[6:7, :]


def mlp_forward_kernel(
    layer,
    rows,
    core_ref,
    middle,
    small,
    up_own,
    up_other,
    down_own,
    down_other,
    result,
    normed,
    hidden,
    slope,
    up_w,
    down_w,
    sems,
):
    core = core_ref[0]
    wait_up = fetch(core, layer, up_own, up_other, up_w, sems.at[0])
    wait_down = fetch(core, layer, down_own, down_other, down_w, sems.at[1])
    norm_rows(middle, normed, small[1:2, :], small[3:4, :], rows)
    wait_up()

    def step(at):
        part = span(at, 256)
        inner = dot(normed[...], up_w[:, part])
        row = 8 + at // 2
        inner = inner + small[pl.ds(row, 1), span(at % 2, 256)]
        below = 0.5 * (1.0 + lax.erf(inner * (0.5**0.5)))
        hidden[:, part] = (inner * below).astype(bf16)
        slope[:, part] = (
            below + inner * (jnp.exp(-0.5 * inner * inner) * ((2 * np.pi) ** -0.5))
        ).astype(bf16)

    loop(FF // 256, step)
    wait_down()
    result[...] = (
        middle[...] + dot(hidden[...], down_w[...]) + small[7:8, :]
    ).astype(result.dtype)


def mlp_backward_kernel(
    layer,
    rows,
    core_ref,
    grad,
    lay,
    middle,
    normed,
    hidden,
    slope,
    small,
    up_own,
    up_other,
    down_own,
    down_other,
    middle_grad,
    sums,
    keep,
    send,
    up_w,
    down_w,
    grads,
    inner_grad,
    grad_in,
    low,
    turned,
    normed_grad,
    sems,
):
    core = core_ref[0]
    wait_up = fetch(core, layer, up_own, up_other, up_w, sems.at[0])
    wait_down = fetch(core, layer, down_own, down_other, down_w, sems.at[1])
    if layer == 1:
        for image in range(rows // CELL):
            grad_in[image * CELL : (image + 1) * CELL, :] = dot(lay[...], grad[image])
    else:
        grad_in = grad
    low[...] = grad_in[...].astype(bf16)
    sums[...] = jnp.zeros(sums.shape, f32)
    sums[2:3, :] = jnp.sum(low[...].astype(f32), 0, keepdims=True)
    turned[...] = normed[...].T
    wait_down()

    def step(at):
        part = span(at, 256)
        back = dot_nt(low[...], down_w[part, :]) * slope[:, part].astype(f32)
        back = back.astype(bf16)
        inner_grad[:, part] = back
        sums[pl.ds(3 + at // 2, 1), span(at % 2, 256)] = jnp.sum(
            back.astype(f32), 0, keepdims=True
        )
        down_grad = dot(hidden[:, part].T, low[...]).astype(bf16)
        grads[at // 4, pl.ds(pl.multiple_of(1024 + (at % 4) * 256, 256), 256), :] = down_grad
        up_grad = dot(turned[...], back).astype(bf16)
        place_at = pl.ds(pl.multiple_of((at // 2) * 256, 256), 256)
        lanes = span(at % 2, 256)
        grads[0, place_at, lanes] = up_grad[:256]
        grads[1, place_at, lanes] = up_grad[256:]

    loop(FF // 256, step)
    wait_up()
    normed_grad[...] = dot_nt(inner_grad[...], up_w[...])
    gain_sum, shift_sum = norm_back(normed_grad, middle, small[1:2, :], grad_in, middle_grad, rows)
    sums[0:1, :] = gain_sum
    sums[1:2, :] = shift_sum
    give(core, grads, keep, send, sems.at[2])


def attention_backward_kernel(
    layer,
    rows,
    core_ref,
    middle_grad,
    source,
    lay,
    unlay,
    to_moved,
    from_moved,
    normed,
    qkv,
    probs,
    mixed,
    small,
    qkv_own,
    qkv_other,
    proj_own,
    proj_other,
    source_grad,
    sums,
    pairs,
    keep,
    send,
    qkv_w,
    proj_w,
    grads,
    tokens_in,
    low,
    mix_grad,
    joined,
    moved_grad,
    turned,
    normed_grad,
    sems,
):
    core = core_ref[0]
    wait_qkv = fetch(core, layer, qkv_own, qkv_other, qkv_w, sems.at[0])
    wait_proj = fetch(core, layer, proj_own, proj_other, proj_w, sems.at[1])
    if layer == 0:
        for image in range(rows // CELL):
            tokens_in[image * CELL : (image + 1) * CELL, :] = dot(lay[...], source[image])
    else:
        tokens_in = source
    low[...] = middle_grad[...].astype(bf16)
    sums[...] = jnp.zeros(sums.shape, f32)
    sums[4:5, :] = jnp.sum(low[...].astype(f32), 0, keepdims=True)
    turned[...] = mixed[...].T
    for side in range(2):
        grads[side, 768:1024, :] = dot(turned[side * 256 : (side + 1) * 256, :], low[...]).astype(
            bf16
        )
    wait_proj()
    if layer == 0:
        mix_grad[...] = dot_nt(low[...], proj_w[...]).astype(bf16)
        target = joined
    else:
        moved_grad[:, :D] = dot_nt(low[...], proj_w[...]).astype(bf16)
        move(to_moved[...], moved_grad, mix_grad, rows, D)
        target = moved_grad
    pairs[...] = jnp.zeros(pairs.shape, f32)
    masks = head_masks()

    def window(at):
        part = span(at, ROWS)
        for quad in range(QUADS):
            queries = stack_heads(qkv[part, quad * 128 : (quad + 1) * 128], masks)
            keys = qkv[part, D + quad * 128 : D + (quad + 1) * 128]
            values = qkv[part, 2 * D + quad * 128 : 2 * D + (quad + 1) * 128]
            given = stack_heads(mix_grad[part, quad * 128 : (quad + 1) * 128], masks)
            prob = probs[at, quad]
            prob_grad = dot_nt(values, given)
            delta = jnp.sum(prob_grad * prob, 0, keepdims=True)
            score_grad = (prob * (prob_grad - delta)).astype(bf16)
            pairs[quad] += score_grad.astype(f32)
            values_grad = dot(prob.astype(bf16), given)
            keys_grad = scale * dot(score_grad, queries)
            queries_grad = scale * pick_heads(dot_tn(score_grad, keys), masks)
            target[part, quad * 128 : (quad + 1) * 128] = queries_grad.astype(bf16)
            target[part, D + quad * 128 : D + (quad + 1) * 128] = keys_grad.astype(bf16)
            target[part, 2 * D + quad * 128 : 2 * D + (quad + 1) * 128] = values_grad.astype(bf16)

    loop(rows // ROWS, window)
    if layer:
        move(from_moved[...], moved_grad, joined, rows, 3 * D)
    sums[2:3, :] = jnp.sum(joined[:, :D].astype(f32), 0, keepdims=True)
    sums[3:4, :] = jnp.sum(joined[:, 2 * D :].astype(f32), 0, keepdims=True)
    turned[...] = normed[...].T
    for at in range(3):
        for side in range(2):
            grads[side, at * 256 : (at + 1) * 256, :] = dot(
                turned[side * 256 : (side + 1) * 256, :], joined[:, at * D : (at + 1) * D]
            ).astype(bf16)
    wait_qkv()
    normed_grad[...] = dot_nt(joined[...], qkv_w[...])
    if layer == 0:
        gain_sum, shift_sum = norm_back(
            normed_grad, tokens_in, small[0:1, :], middle_grad, normed_grad, rows
        )
        for image in range(rows // CELL):
            value = normed_grad[image * CELL : (image + 1) * CELL, :]
            high = value.astype(bf16)
            rest = value - high.astype(f32)
            fine = rest.astype(bf16)
            last = (rest - fine.astype(f32)).astype(bf16)
            source_grad[image] = (
                dot(unlay[...], high) + dot(unlay[...], fine) + dot(unlay[...], last)
            )
    else:
        gain_sum, shift_sum = norm_back(
            normed_grad, tokens_in, small[0:1, :], middle_grad, source_grad, rows
        )
    sums[0:1, :] = gain_sum
    sums[1:2, :] = shift_sum
    give(core, grads, keep, send, sems.at[2])


def call(kernel, layer, rows, core, inputs, kinds, outs, out_kinds, scratch, flops):
    spaces = {"v": pltpu.VMEM, "a": pl.ANY}
    moved = sum(item.size * item.dtype.itemsize for item in inputs)
    return pl.pallas_call(
        functools.partial(kernel, layer, rows),
        in_specs=[pl.BlockSpec(memory_space=pltpu.SMEM)]
        + [pl.BlockSpec(memory_space=spaces[kind]) for kind in kinds],
        out_specs=[pl.BlockSpec(memory_space=spaces[kind]) for kind in out_kinds],
        out_shape=outs,
        scratch_shapes=scratch,
        compiler_params=pltpu.CompilerParams(vmem_limit_bytes=56 * 1024 * 1024),
        cost_estimate=pl.CostEstimate(flops=flops, bytes_accessed=moved, transcendentals=0),
        name=kernel.__name__ + str(layer),
    )(core, *inputs)


def shape(dims, dtype):
    return jax.ShapeDtypeStruct(dims, dtype)


def swap_cores(value):
    return lax.ppermute(value, "fsdp", [(0, 1), (1, 0)])


def in_order(own, other, axis):
    first = lax.axis_index("fsdp") == 0
    return jnp.concatenate([jnp.where(first, own, other), jnp.where(first, other, own)], axis=axis)


def add_low(one, two):
    return (one.astype(f32) + two.astype(f32)).astype(bf16)


def dp_bit(bit):
    return (lax.axis_index("dp") >> bit) & 1


def dp_swap(value, bit, count):
    return lax.ppermute(value, "dp", [(at, at ^ (1 << bit)) for at in range(count)])


def halve(value, bit, count):
    half = value.shape[0] // 2
    side = dp_bit(bit)
    keep = lax.dynamic_slice_in_dim(value, side * half, half, 0)
    send = lax.dynamic_slice_in_dim(value, (1 - side) * half, half, 0)
    return add_low(keep, dp_swap(send, bit, count))


def unhalve(value, bit, count):
    other = dp_swap(value, bit, count)
    first = dp_bit(bit) == 0
    return jnp.concatenate([jnp.where(first, value, other), jnp.where(first, other, value)], axis=0)


def dp_reduce(bucket, count):
    bits = count.bit_length() - 1
    half = bucket.shape[0] // 2
    done = []
    for piece, order in ((bucket[:half], (0, 1)), (bucket[half:], (1, 0))):
        for bit in order:
            piece = halve(piece, bit, count)
        for bit in range(2, bits):
            piece = add_low(piece, dp_swap(piece, bit, count))
        for bit in order[::-1]:
            piece = unhalve(piece, bit, count)
        done.append(piece)
    return jnp.concatenate(done, axis=0)


def dp_sum(value, count):
    for bit in range(count.bit_length() - 1):
        value = value + dp_swap(value, bit, count)
    return value


def rows_to_columns(value, rows):
    return jnp.concatenate([value[at : at + rows] for at in range(0, value.shape[0], rows)], axis=1)


def body(
    tokens,
    regions,
    rel_index,
    norm_gains,
    norm_shifts,
    qkv_weight,
    qv_bias,
    rel_table,
    proj_weight,
    proj_bias,
    fc1_weight,
    fc1_bias,
    fc2_weight,
    fc2_bias,
    cotangent,
):
    count = lax.axis_size("dp")
    images = tokens.shape[0]
    rows = images * CELL
    windows = images * 4
    own_small = jnp.concatenate(
        [
            norm_gains,
            norm_shifts,
            qv_bias,
            proj_bias[:, None],
            fc2_bias[:, None],
            fc1_bias.reshape(2, 4, D // 2),
        ],
        axis=1,
    )
    own_table = rel_table
    qkv_other = swap_cores(qkv_weight)
    proj_other = swap_cores(proj_weight)
    other_small = swap_cores(own_small)
    other_table = swap_cores(own_table)
    up_other = swap_cores(fc1_weight)
    down_other = swap_cores(fc2_weight)

    core = lax.axis_index("fsdp").astype(jnp.int32).reshape(1)
    eight = in_order(own_small[:, :8], other_small[:, :8], 2)
    four = in_order(
        own_small[:, 8:].reshape(2, 2, D), other_small[:, 8:].reshape(2, 2, D), 1
    )
    small_all = jnp.concatenate([eight, four, jnp.zeros((2, 4, D), bf16)], axis=1).astype(f32)
    table = in_order(own_table, other_table, 2)
    table = jnp.concatenate(
        [table, jnp.full((2, 1, HEADS), -1e30, bf16), jnp.zeros((2, LIVE - RELS - 1, HEADS), bf16)],
        axis=1,
    )
    grid_index = rel_index.reshape(WT, WT).T
    grid_index = jnp.pad(grid_index, ((0, 0), (0, ROWS - WT)))
    grid_index = jnp.pad(grid_index, ((0, ROWS - WT), (0, 0)), constant_values=RELS)
    onehot = (
        grid_index.reshape(1, ROWS * ROWS) == jnp.arange(LIVE, dtype=jnp.int32)[:, None]
    ).astype(bf16)
    bias_all = jnp.einsum("lrh,rp->lhp", table, onehot, preferred_element_type=f32)
    bias_all = (
        bias_all.reshape(2, QUADS, 4, ROWS, ROWS)
        .transpose(0, 1, 3, 2, 4)
        .reshape(2, QUADS, ROWS, 4 * ROWS)
    )
    region_win = (
        regions.reshape(2, WIN, 2, WIN).transpose(0, 2, 1, 3).reshape(4, WT)
    )
    mask = jnp.where(region_win[:, :, None] == region_win[:, None, :], 0.0, -100.0).astype(f32)
    mask = jnp.pad(mask, ((0, 0), (0, ROWS - WT), (0, ROWS - WT)))
    mask = jnp.tile(mask, (1, 1, 4))
    lay, unlay, to_moved, from_moved = [jnp.asarray(item, bf16) for item in permutations()]

    vmem = pltpu.VMEM
    wide = (rows, D)
    attn_w = [vmem((D, 3 * D), bf16), vmem((D, D), bf16)]
    mlp_w = [vmem((D, FF), bf16), vmem((FF, D), bf16)]
    two_sems = pltpu.SemaphoreType.DMA((2, 2))
    three_sems = pltpu.SemaphoreType.DMA((3, 2))
    attn_flops = 2 * rows * D * D * 5
    mlp_flops = 2 * rows * D * FF * 2
    current = tokens
    saved = []
    for layer in range(2):
        small = small_all[layer]
        middle, normed, qkv, probs, mixed = call(
            attention_forward_kernel,
            layer,
            rows,
            core,
            [
                current,
                lay,
                to_moved,
                from_moved,
                small,
                bias_all[layer],
                mask,
                qkv_weight,
                qkv_other,
                proj_weight,
                proj_other,
            ],
            "vvvvvvvaaaa",
            [
                shape(wide, f32),
                shape(wide, bf16),
                shape((rows, 3 * D), bf16),
                shape((windows, QUADS, ROWS, 4 * ROWS), f32),
                shape(wide, bf16),
            ],
            "vvvvv",
            attn_w + [vmem(wide if layer == 0 else (8, 128), f32), vmem(wide, bf16), two_sems],
            attn_flops,
        )
        result, normed_two, hidden, slope = call(
            mlp_forward_kernel,
            layer,
            rows,
            core,
            [middle, small, fc1_weight, up_other, fc2_weight, down_other],
            "vvaaaa",
            [
                shape(wide, f32),
                shape(wide, bf16),
                shape((rows, FF), bf16),
                shape((rows, FF), bf16),
            ],
            "vvvv",
            mlp_w + [two_sems],
            mlp_flops,
        )
        saved.append((current, middle, normed, qkv, probs, mixed, normed_two, hidden, slope, small))
        current = result
    grad = cotangent
    kept = [None, None]
    small_sums = [None, None]
    pair_sums = [None, None]
    for layer in (1, 0):
        source, middle, normed, qkv, probs, mixed, normed_two, hidden, slope, small = saved[layer]
        middle_grad, mlp_sums, mlp_keep, mlp_send = call(
            mlp_backward_kernel,
            layer,
            rows,
            core,
            [
                grad,
                lay,
                middle,
                normed_two,
                hidden,
                slope,
                small,
                fc1_weight,
                up_other,
                fc2_weight,
                down_other,
            ],
            "vvvvvvvaaaa",
            [
                shape(wide, f32),
                shape((8, D), f32),
                shape((FF, D), bf16),
                shape((FF, D), bf16),
            ],
            "vvaa",
            mlp_w
            + [
                vmem((2, FF, D), bf16),
                vmem((rows, FF), bf16),
                vmem(wide if layer == 1 else (8, 128), f32),
                vmem(wide, bf16),
                vmem((D, rows), bf16),
                vmem(wide, f32),
                three_sems,
            ],
            2 * mlp_flops,
        )
        mlp_bucket = dp_reduce(add_low(mlp_keep, swap_cores(mlp_send)), count)
        grad, attn_sums, pairs, attn_keep, attn_send = call(
            attention_backward_kernel,
            layer,
            rows,
            core,
            [
                middle_grad,
                source,
                lay,
                unlay,
                to_moved,
                from_moved,
                normed,
                qkv,
                probs,
                mixed,
                small,
                qkv_weight,
                qkv_other,
                proj_weight,
                proj_other,
            ],
            "vvvvvvvvvvvaaaa",
            [
                shape(wide if layer else (images, PIX, D), f32),
                shape((8, D), f32),
                shape((QUADS, ROWS, 4 * ROWS), f32),
                shape((2 * D, D), bf16),
                shape((2 * D, D), bf16),
            ],
            "vvvaa",
            attn_w
            + [
                vmem((2, 2 * D, D), bf16),
                vmem(wide if layer == 0 else (8, 128), f32),
                vmem(wide, bf16),
                vmem(wide, bf16),
                vmem((rows, 3 * D), bf16),
                vmem((rows, 3 * D) if layer else (16, 128), bf16),
                vmem((D, rows), bf16),
                vmem(wide, f32),
                three_sems,
            ],
            2 * attn_flops,
        )
        attn_bucket = dp_reduce(add_low(attn_keep, swap_cores(attn_send)), count)
        kept[layer] = (mlp_bucket, attn_bucket)
        small_sums[layer] = jnp.concatenate([attn_sums, mlp_sums], axis=0)
        pair_sums[layer] = pairs
    output = lax.reduce_precision(current, 8, 7).astype(bf16)
    output = (
        output.reshape(images, 2, 2, ROWS, D)[:, :, :, :WT]
        .reshape(images, 2, 2, WIN, WIN, D)
        .transpose(0, 1, 3, 2, 4, 5)
        .reshape(images, PIX, D)
    )
    pair_flat = (
        jnp.stack(pair_sums)
        .reshape(2, QUADS, ROWS, 4, ROWS)
        .transpose(0, 1, 3, 2, 4)
        .reshape(2, HEADS, ROWS * ROWS)
    )
    table_sums = jnp.einsum(
        "lhp,rp->lrh", pair_flat, onehot.astype(f32), precision=lax.Precision.HIGHEST
    )[:, :RELS]
    table_rows = jnp.pad(table_sums.reshape(2, RELS * HEADS), ((0, 0), (0, -RELS * HEADS % D)))
    packed = jnp.concatenate(
        [small_sums[0], small_sums[1], table_rows.reshape(-1, D)], axis=0
    )
    packed = dp_sum(packed + swap_cores(packed), count)
    at_core = lax.axis_index("fsdp")

    def half_of(value):
        half = value.shape[-1] // 2
        return lax.dynamic_slice_in_dim(value, at_core * half, half, value.ndim - 1)

    sums = packed[:32].reshape(2, 16, D)
    gains_g = half_of(sums[:, 0:9:8])
    shifts_g = half_of(sums[:, 1:10:8])
    qv_g = half_of(sums[:, 2:4])
    proj_b_g = half_of(sums[:, 4])
    down_b_g = half_of(sums[:, 10])
    up_b_g = half_of(sums[:, 11:15].reshape(2, FF))
    table_g = half_of(
        packed[32:].reshape(2, -1)[:, : RELS * HEADS].reshape(2, RELS, HEADS)
    )
    big = [[], [], [], []]
    for layer in range(2):
        mlp, attn = kept[layer]
        part = D // 2
        big[0].append(rows_to_columns(attn[: 3 * part], part))
        big[1].append(attn[3 * part :])
        big[2].append(rows_to_columns(mlp[: 4 * part], part))
        big[3].append(mlp[4 * part :])
    qkv_g, proj_g, up_g, down_g = [jnp.stack(item).astype(f32) for item in big]
    return (
        output,
        grad,
        gains_g,
        shifts_g,
        qkv_g,
        qv_g,
        table_g,
        proj_g,
        proj_b_g,
        up_g,
        up_b_g,
        down_g,
        down_b_g,
    )


def solution(mesh):
    return jax.shard_map(
        body,
        mesh=mesh,
        in_specs=(
            P(("dp", "fsdp"), None, None),
            P(),
            P(),
            P(None, None, "fsdp"),
            P(None, None, "fsdp"),
            P(None, "fsdp", None),
            P(None, None, "fsdp"),
            P(None, None, "fsdp"),
            P(None, "fsdp", None),
            P(None, "fsdp"),
            P(None, "fsdp", None),
            P(None, "fsdp"),
            P(None, "fsdp", None),
            P(None, "fsdp"),
            P(("dp", "fsdp"), None, None),
        ),
        out_specs=(
            P(("dp", "fsdp"), None, None),
            P(("dp", "fsdp"), None, None),
            P(None, None, "fsdp"),
            P(None, None, "fsdp"),
            P(None, "fsdp", None),
            P(None, None, "fsdp"),
            P(None, None, "fsdp"),
            P(None, "fsdp", None),
            P(None, "fsdp"),
            P(None, "fsdp", None),
            P(None, "fsdp"),
            P(None, "fsdp", None),
            P(None, "fsdp"),
        ),
        check_vma=False,
    )
```

```python
import functools

import numpy as np

import jax
import jax.numpy as jnp
from jax import lax
from jax.experimental import pallas as pl
from jax.experimental.pallas import tpu as pltpu
from jax.sharding import PartitionSpec as P

D = 512
HEADS = 16
HD = 32
FF = 2048
WIN = 7
IMG = 14
SHIFT = 3
PIX = 196
WT = 49
RELS = 169
ROWS = 64
CELL = 256
QUADS = 4
TIE = 0
LIVE = 176

norm_eps = 1e-05
scale = HD**-0.5
f32 = jnp.float32
bf16 = jnp.bfloat16


def place(offset):
    rows = np.full((CELL,), -1, np.int64)
    for i in range(IMG):
        for j in range(IMG):
            window = (i // WIN) * 2 + j // WIN
            row = window * ROWS + (i % WIN) * WIN + j % WIN
            rows[row] = ((i + offset) % IMG) * IMG + (j + offset) % IMG
    return rows


def permutations():
    base, moved = place(0), place(SHIFT)
    lay = np.zeros((CELL, PIX), np.float32)
    lay[base >= 0, base[base >= 0]] = 1
    shifted = np.zeros((CELL, PIX), np.float32)
    shifted[moved >= 0, moved[moved >= 0]] = 1
    return lay, lay.T.copy(), shifted @ lay.T, lay @ shifted.T


def dot(a, b):
    return jnp.dot(a, b, preferred_element_type=f32)


def dot_nt(a, b):
    return lax.dot_general(a, b, (((1,), (1,)), ((), ())), preferred_element_type=f32)


def dot_tn(a, b):
    return lax.dot_general(a, b, (((0,), (0,)), ((), ())), preferred_element_type=f32)


def loop(count, step):
    def run(at, carry):
        step(at)
        return carry

    lax.fori_loop(0, count, run, 0)


def span(at, size):
    return pl.ds(pl.multiple_of(at * size, size), size)


def normal(values):
    centred = values - jnp.mean(values, -1, keepdims=True)
    spread = lax.rsqrt(jnp.mean(centred * centred, -1, keepdims=True) + norm_eps)
    return centred * spread, spread


def norm_rows(source, target, gain, shift, rows):
    def step(at):
        part = span(at, 128)
        unit, _ = normal(source[part, :])
        target[part, :] = (unit * gain + shift).astype(bf16)

    loop(rows // 128, step)


def norm_back(grad, source, gain, extra, target, rows):
    def step(at, sums):
        part = span(at, 128)
        dh = grad[part, :]
        unit, spread = normal(source[part, :])
        du = dh * gain
        back = spread * (
            du
            - jnp.mean(du, -1, keepdims=True)
            - unit * jnp.mean(du * unit, -1, keepdims=True)
        )
        target[part, :] = extra[part, :] + back
        return (
            sums[0] + jnp.sum(dh * unit, 0, keepdims=True),
            sums[1] + jnp.sum(dh, 0, keepdims=True),
        )

    zero = jnp.zeros((1, D), f32)
    return lax.fori_loop(0, rows // 128, step, (zero, zero))


def move(matrix, source, target, rows, columns):
    for image in range(rows // CELL):
        for at in range(columns // D):
            target[image * CELL : (image + 1) * CELL, at * D : (at + 1) * D] = dot(
                matrix, source[image * CELL : (image + 1) * CELL, at * D : (at + 1) * D]
            ).astype(bf16)


def fetch(core, layer, own, other, target, sems):
    half = own.shape[1]
    mine = pltpu.make_async_copy(
        own.at[layer], target.at[pl.ds(pl.multiple_of(core * half, half), half), :], sems.at[0]
    )
    theirs = pltpu.make_async_copy(
        other.at[layer],
        target.at[pl.ds(pl.multiple_of((1 - core) * half, half), half), :],
        sems.at[1],
    )
    mine.start()
    theirs.start()

    def wait():
        mine.wait()
        theirs.wait()

    return wait


def give(core, grads, keep, send, sems):
    one = pltpu.make_async_copy(grads.at[core], keep, sems.at[0])
    two = pltpu.make_async_copy(grads.at[1 - core], send, sems.at[1])
    one.start()
    two.start()
    one.wait()
    two.wait()


def head_masks():
    lanes = lax.broadcasted_iota(jnp.int32, (ROWS, 128), 1) // HD
    return [lanes == at for at in range(QUADS)]


def stack_heads(value, masks):
    zero = jnp.zeros_like(value)
    return jnp.concatenate([jnp.where(mask, value, zero) for mask in masks], axis=0)


def pick_heads(value, masks):
    result = value[:ROWS]
    for at in range(1, QUADS):
        result = jnp.where(masks[at], value[at * ROWS : (at + 1) * ROWS], result)
    return result


def attention_forward_kernel(
    layer,
    rows,
    core_ref,
    source,
    lay,
    to_moved,
    from_moved,
    small,
    bias,
    mask,
    qkv_own,
    qkv_other,
    proj_own,
    proj_other,
    middle,
    normed,
    qkv,
    probs,
    mixed,
    qkv_w,
    proj_w,
    tokens_in,
    work,
    sems,
):
    core = core_ref[0]
    wait_qkv = fetch(core, layer, qkv_own, qkv_other, qkv_w, sems.at[0])
    wait_proj = fetch(core, layer, proj_own, proj_other, proj_w, sems.at[1])
    if layer == 0:
        for image in range(rows // CELL):
            tokens_in[image * CELL : (image + 1) * CELL, :] = dot(lay[...], source[image])
    else:
        tokens_in = source
    norm_rows(tokens_in, normed, small[0:1, :], small[2:3, :], rows)
    if layer == 0:
        moved = normed
    else:
        move(to_moved[...], normed, work, rows, D)
        moved = work
    wait_qkv()
    for at in range(3):
        part = dot(moved[...], qkv_w[:, at * D : (at + 1) * D])
        if at == 0:
            part = part + small[4:5, :]
        if at == 2:
            part = part + small[5:6, :]
        qkv[:, at * D : (at + 1) * D] = part.astype(bf16)
    masks = head_masks()
    out = mixed if layer == 0 else work

    def window(at):
        part = span(at, ROWS)
        for quad in range(QUADS):
            lanes = slice(quad * 128, (quad + 1) * 128)
            queries = stack_heads(qkv[part, lanes], masks)
            keys = qkv[part, D + quad * 128 : D + (quad + 1) * 128]
            values = qkv[part, 2 * D + quad * 128 : 2 * D + (quad + 1) * 128]
            scores = scale * dot_nt(keys, queries) + bias[quad]
            if layer:
                scores = scores + mask[at % 4]
            expo = jnp.exp(scores - jnp.max(scores, 0, keepdims=True))
            prob = expo / jnp.sum(expo, 0, keepdims=True)
            probs[at, quad] = prob
            mix = dot_tn(prob.astype(bf16), values)
            out[part, lanes] = pick_heads(mix, masks).astype(bf16)

    loop(rows // ROWS, window)
    if layer:
        move(from_moved[...], work, mixed, rows, D)
    wait_proj()
    middle[...] = tokens_in[...] + dot(mixed[...], proj_w[...]) + small[6:7, :]


def mlp_forward_kernel(
    layer,
    rows,
    core_ref,
    middle,
    small,
    up_own,
    up_other,
    down_own,
    down_other,
    result,
    normed,
    hidden,
    slope,
    up_w,
    down_w,
    sems,
):
    core = core_ref[0]
    wait_up = fetch(core, layer, up_own, up_other, up_w, sems.at[0])
    wait_down = fetch(core, layer, down_own, down_other, down_w, sems.at[1])
    norm_rows(middle, normed, small[1:2, :], small[3:4, :], rows)
    wait_up()

    def step(at):
        part = span(at, 256)
        inner = dot(normed[...], up_w[:, part])
        row = 8 + at // 2
        inner = inner + small[pl.ds(row, 1), span(at % 2, 256)]
        below = 0.5 * (1.0 + lax.erf(inner * (0.5**0.5)))
        hidden[:, part] = (inner * below).astype(bf16)
        slope[:, part] = (
            below + inner * (jnp.exp(-0.5 * inner * inner) * ((2 * np.pi) ** -0.5))
        ).astype(bf16)

    loop(FF // 256, step)
    wait_down()
    result[...] = (
        middle[...] + dot(hidden[...], down_w[...]) + small[7:8, :]
    ).astype(result.dtype)


def mlp_backward_kernel(
    layer,
    rows,
    core_ref,
    grad,
    lay,
    middle,
    normed,
    hidden,
    slope,
    small,
    up_own,
    up_other,
    down_own,
    down_other,
    middle_grad,
    sums,
    keep,
    send,
    up_w,
    down_w,
    grads,
    inner_grad,
    grad_in,
    low,
    turned,
    normed_grad,
    sems,
):
    core = core_ref[0]
    wait_up = fetch(core, layer, up_own, up_other, up_w, sems.at[0])
    wait_down = fetch(core, layer, down_own, down_other, down_w, sems.at[1])
    if layer == 1:
        for image in range(rows // CELL):
            grad_in[image * CELL : (image + 1) * CELL, :] = dot(lay[...], grad[image])
    else:
        grad_in = grad
    low[...] = grad_in[...].astype(bf16)
    sums[...] = jnp.zeros(sums.shape, f32)
    sums[2:3, :] = jnp.sum(low[...].astype(f32), 0, keepdims=True)
    turned[...] = normed[...].T
    wait_down()

    def step(at):
        part = span(at, 256)
        back = dot_nt(low[...], down_w[part, :]) * slope[:, part].astype(f32)
        back = back.astype(bf16)
        inner_grad[:, part] = back
        sums[pl.ds(3 + at // 2, 1), span(at % 2, 256)] = jnp.sum(
            back.astype(f32), 0, keepdims=True
        )
        down_grad = dot(hidden[:, part].T, low[...]).astype(bf16)
        grads[at // 4, pl.ds(pl.multiple_of(1024 + (at % 4) * 256, 256), 256), :] = down_grad
        up_grad = dot(turned[...], back).astype(bf16)
        place_at = pl.ds(pl.multiple_of((at // 2) * 256, 256), 256)
        lanes = span(at % 2, 256)
        grads[0, place_at, lanes] = up_grad[:256]
        grads[1, place_at, lanes] = up_grad[256:]

    loop(FF // 256, step)
    wait_up()
    normed_grad[...] = dot_nt(inner_grad[...], up_w[...])
    gain_sum, shift_sum = norm_back(normed_grad, middle, small[1:2, :], grad_in, middle_grad, rows)
    sums[0:1, :] = gain_sum
    sums[1:2, :] = shift_sum
    give(core, grads, keep, send, sems.at[2])


def attention_backward_kernel(
    layer,
    rows,
    core_ref,
    middle_grad,
    source,
    lay,
    unlay,
    to_moved,
    from_moved,
    normed,
    qkv,
    probs,
    mixed,
    small,
    qkv_own,
    qkv_other,
    proj_own,
    proj_other,
    source_grad,
    sums,
    pairs,
    keep,
    send,
    qkv_w,
    proj_w,
    grads,
    tokens_in,
    low,
    mix_grad,
    joined,
    moved_grad,
    turned,
    normed_grad,
    sems,
):
    core = core_ref[0]
    wait_qkv = fetch(core, layer, qkv_own, qkv_other, qkv_w, sems.at[0])
    wait_proj = fetch(core, layer, proj_own, proj_other, proj_w, sems.at[1])
    if layer == 0:
        for image in range(rows // CELL):
            tokens_in[image * CELL : (image + 1) * CELL, :] = dot(lay[...], source[image])
    else:
        tokens_in = source
    low[...] = middle_grad[...].astype(bf16)
    sums[...] = jnp.zeros(sums.shape, f32)
    sums[4:5, :] = jnp.sum(low[...].astype(f32), 0, keepdims=True)
    turned[...] = mixed[...].T
    for side in range(2):
        grads[side, 768:1024, :] = dot(turned[side * 256 : (side + 1) * 256, :], low[...]).astype(
            bf16
        )
    wait_proj()
    if layer == 0:
        mix_grad[...] = dot_nt(low[...], proj_w[...]).astype(bf16)
        target = joined
    else:
        moved_grad[:, :D] = dot_nt(low[...], proj_w[...]).astype(bf16)
        move(to_moved[...], moved_grad, mix_grad, rows, D)
        target = moved_grad
    pairs[...] = jnp.zeros(pairs.shape, f32)
    masks = head_masks()

    def window(at):
        part = span(at, ROWS)
        for quad in range(QUADS):
            queries = stack_heads(qkv[part, quad * 128 : (quad + 1) * 128], masks)
            keys = qkv[part, D + quad * 128 : D + (quad + 1) * 128]
            values = qkv[part, 2 * D + quad * 128 : 2 * D + (quad + 1) * 128]
            given = stack_heads(mix_grad[part, quad * 128 : (quad + 1) * 128], masks)
            prob = probs[at, quad]
            prob_grad = dot_nt(values, given)
            delta = jnp.sum(prob_grad * prob, 0, keepdims=True)
            score_grad = (prob * (prob_grad - delta)).astype(bf16)
            pairs[quad] += score_grad.astype(f32)
            values_grad = dot(prob.astype(bf16), given)
            keys_grad = scale * dot(score_grad, queries)
            queries_grad = scale * pick_heads(dot_tn(score_grad, keys), masks)
            target[part, quad * 128 : (quad + 1) * 128] = queries_grad.astype(bf16)
            target[part, D + quad * 128 : D + (quad + 1) * 128] = keys_grad.astype(bf16)
            target[part, 2 * D + quad * 128 : 2 * D + (quad + 1) * 128] = values_grad.astype(bf16)

    loop(rows // ROWS, window)
    if layer:
        move(from_moved[...], moved_grad, joined, rows, 3 * D)
    sums[2:3, :] = jnp.sum(joined[:, :D].astype(f32), 0, keepdims=True)
    sums[3:4, :] = jnp.sum(joined[:, 2 * D :].astype(f32), 0, keepdims=True)
    turned[...] = normed[...].T
    for at in range(3):
        for side in range(2):
            grads[side, at * 256 : (at + 1) * 256, :] = dot(
                turned[side * 256 : (side + 1) * 256, :], joined[:, at * D : (at + 1) * D]
            ).astype(bf16)
    wait_qkv()
    normed_grad[...] = dot_nt(joined[...], qkv_w[...])
    if layer == 0:
        gain_sum, shift_sum = norm_back(
            normed_grad, tokens_in, small[0:1, :], middle_grad, normed_grad, rows
        )
        for image in range(rows // CELL):
            value = normed_grad[image * CELL : (image + 1) * CELL, :]
            high = value.astype(bf16)
            rest = value - high.astype(f32)
            fine = rest.astype(bf16)
            last = (rest - fine.astype(f32)).astype(bf16)
            source_grad[image] = (
                dot(unlay[...], high) + dot(unlay[...], fine) + dot(unlay[...], last)
            )
    else:
        gain_sum, shift_sum = norm_back(
            normed_grad, tokens_in, small[0:1, :], middle_grad, source_grad, rows
        )
    sums[0:1, :] = gain_sum
    sums[1:2, :] = shift_sum
    give(core, grads, keep, send, sems.at[2])


def call(kernel, layer, rows, core, inputs, kinds, outs, out_kinds, scratch, flops):
    spaces = {"v": pltpu.VMEM, "a": pl.ANY}
    return pl.pallas_call(
        functools.partial(kernel, layer, rows),
        in_specs=[pl.BlockSpec(memory_space=pltpu.SMEM)]
        + [pl.BlockSpec(memory_space=spaces[kind]) for kind in kinds],
        out_specs=[pl.BlockSpec(memory_space=spaces[kind]) for kind in out_kinds],
        out_shape=outs,
        scratch_shapes=scratch,
        compiler_params=pltpu.CompilerParams(vmem_limit_bytes=56 * 1024 * 1024),
        cost_estimate=pl.CostEstimate(flops=1, bytes_accessed=1, transcendentals=0),
        name=kernel.__name__ + str(layer),
    )(core, *inputs)


def shape(dims, dtype):
    return jax.ShapeDtypeStruct(dims, dtype)


def swap_cores(value):
    return lax.ppermute(value, "fsdp", [(0, 1), (1, 0)])


def in_order(own, other, axis):
    first = lax.axis_index("fsdp") == 0
    return jnp.concatenate([jnp.where(first, own, other), jnp.where(first, other, own)], axis=axis)


def dp_swap(value, bit, count):
    return lax.ppermute(value, "dp", [(at, at ^ (1 << bit)) for at in range(count)])


def plus(one, two):
    return (one.astype(f32) + two.astype(f32)).astype(bf16)


def op_first(bits, ins, outs):
    quarter = outs[0].shape[0] // 2
    for part in range(2):
        keep, got = ins[2 * part : 2 * part + 2]
        send, hold = outs[2 * part : 2 * part + 2]
        side = bits[part]
        for low in range(2):
            rows = slice(low * quarter, (low + 1) * quarter)
            send[rows, :] = plus(keep[2 * (1 - side) + low], got[2 * (1 - side) + low])
            hold[rows, :] = plus(keep[2 * side + low], got[2 * side + low])


def op_first_small(bits, ins, outs):
    quarter = outs[0].shape[0] // 2
    rows_in = quarter - 16
    tiny, tiny_got = ins[4:6]
    for part in range(2):
        keep, got = ins[2 * part : 2 * part + 2]
        send, hold = outs[2 * part : 2 * part + 2]
        side = bits[part]
        for low in range(2):
            first = slice(low * quarter, low * quarter + rows_in)
            last = slice(low * quarter + rows_in, (low + 1) * quarter)
            for target, at in ((send, 2 * (1 - side) + low), (hold, 2 * side + low)):
                target[first, :] = plus(keep[at], got[at])
                target[last, :] = plus(tiny[4 * part + at], tiny_got[4 * part + at])


def op_second(bits, ins, outs):
    for part in range(2):
        hold, got = ins[2 * part : 2 * part + 2]
        send, rest = outs[2 * part : 2 * part + 2]
        side = bits[1 - part]
        send[...] = plus(hold[1 - side], got[1 - side])
        rest[...] = plus(hold[side], got[side])


def op_join(bits, ins, outs):
    quarter = ins[0].shape[0]
    for part in range(2):
        outs[0][part * quarter : (part + 1) * quarter, :] = plus(
            ins[2 * part][...], ins[2 * part + 1][...]
        )


def op_add(bits, ins, outs):
    outs[0][...] = plus(ins[0][...], ins[1][...])


def step_kernel(plan, bits_ref, *refs):
    bits = (bits_ref[0], bits_ref[1])
    total = sum(item[1] for item in plan)
    ins, outs = refs[:total], refs[total:]
    for op, inputs, outputs in plan:
        op(bits, ins[:inputs], outs[:outputs])
        ins, outs = ins[inputs:], outs[outputs:]


class Group:
    def __init__(self, rows, parts, count, tiny=None):
        self.small = tiny
        self.quarter = rows // 4 + (16 if tiny else 0)
        self.parts = parts
        self.count = count
        self.stage = 0
        self.later = count.bit_length() - 3
        self.done = False

    def low(self, rows):
        return shape((rows, D), bf16)

    def next_op(self):
        q = self.quarter
        if self.stage == 0:
            ins = [item.reshape(4, -1, D) for pair in self.parts for item in pair]
            if self.small:
                ins += [item.reshape(8, 16, D) for item in self.small]
            return op_first_small if self.small else op_first, ins, [self.low(2 * q)] * 4
        if self.stage == 1:
            ins = [item.reshape(2, q, D) for item in self.state]
            return op_second, ins, [self.low(q)] * 4
        if self.stage == 2:
            return op_join, self.state, [self.low(2 * q)]
        if self.stage < 3 + self.later:
            return op_add, self.state, [self.low(2 * q)]
        return None

    def send(self, outs):
        if self.stage < 2:
            first, second = (0, 1) if self.stage == 0 else (1, 0)
            self.state = [
                outs[1],
                dp_swap(outs[0], first, self.count),
                outs[3],
                dp_swap(outs[2], second, self.count),
            ]
        elif self.stage < 2 + self.later:
            self.state = [outs[0], dp_swap(outs[0], self.stage, self.count)]
        elif self.stage == 2 + self.later:
            mine = outs[0]
            self.state = [mine, dp_swap(mine, 0, self.count), dp_swap(mine, 1, self.count)]
        else:
            q = self.quarter
            mine, by_x, by_y = self.state
            self.state = [
                mine,
                by_x,
                by_y,
                dp_swap(by_x[:q], 1, self.count),
                dp_swap(by_y[q:], 0, self.count),
            ]
            self.done = True
        self.stage += 1


def after(first, then):
    return lax.optimization_barrier((first, then))[1]


def advance(groups, bits, when, final=False):
    ops, marks = [], []
    for group in groups:
        op = group.next_op()
        if op is None:
            group.state = list(after(when, group.state))
            group.send(None)
        else:
            ops.append((group, op))
    if not ops:
        return when
    plan = tuple((op[0], len(op[1]), len(op[2])) for _, op in ops)
    inputs = [item for _, op in ops for item in op[1]]
    outs = [item for _, op in ops for item in op[2]]
    inputs = after(when, inputs)
    results = pl.pallas_call(
        functools.partial(step_kernel, plan),
        in_specs=[pl.BlockSpec(memory_space=pltpu.SMEM)]
        + [pl.BlockSpec(memory_space=pltpu.VMEM)] * len(inputs),
        out_specs=[pl.BlockSpec(memory_space=pltpu.VMEM)] * len(outs),
        out_shape=outs,
        compiler_params=pltpu.CompilerParams(vmem_limit_bytes=56 * 1024 * 1024),
        cost_estimate=pl.CostEstimate(flops=1, bytes_accessed=1, transcendentals=0),
        name="reduce_step",
    )(bits, *inputs)
    for group, op in ops:
        mine, results = results[: len(op[2])], results[len(op[2]) :]
        group.send(mine)
        marks.append(mine[0])
    return marks[0]


def merge_kernel(*refs):
    out = refs[-1]
    start = 0
    for at in range(0, len(refs) - 1, 2):
        rows = refs[at].shape[0]
        out[start : start + rows, :] = plus(refs[at][...], refs[at + 1][...])
        start += rows


def quarters(ins, x, y, target):
    mine, by_x, by_y, far_first, far_second = ins
    q = far_first.shape[0]
    target[x * 2 + y] = mine[:q, :]
    target[(1 - x) * 2 + y] = by_x[:q, :]
    target[x * 2 + 1 - y] = by_y[:q, :]
    target[(1 - x) * 2 + 1 - y] = far_first[...]
    target[4 + y * 2 + x] = mine[q:, :]
    target[4 + y * 2 + 1 - x] = by_x[q:, :]
    target[4 + (1 - y) * 2 + x] = by_y[q:, :]
    target[4 + (1 - y) * 2 + 1 - x] = far_second[...]


def unpack_kernel(bits_ref, *refs):
    x, y, core = bits_ref[0], bits_ref[1], bits_ref[2]
    mlp_in, attn_in, upper = refs[:5], refs[5:10], refs[10]
    qkv_out, proj_out, up_out, down_out = refs[11:15]
    gains_out, shifts_out, qv_out, proj_b_out, up_b_out, down_b_out, table_out = refs[15:22]
    mlp, attn, tiny = refs[22:]
    half = D // 2
    for at in range(2):
        up_out[1, :, 2 * at * D : (2 * at + 1) * D] = upper[2 * at * half : (2 * at + 1) * half, :].astype(f32)
        up_out[1, :, (2 * at + 1) * D : (2 * at + 2) * D] = upper[
            (2 * at + 1) * half : (2 * at + 2) * half, :
        ].astype(f32)
    down_out[1] = upper[2 * D : 4 * D, :].astype(f32)
    for at in range(3):
        qkv_out[1, :, at * D : (at + 1) * D] = upper[
            4 * D + at * half : 4 * D + (at + 1) * half, :
        ].astype(f32)
    proj_out[1] = upper[4 * D + 3 * half : 6 * D, :].astype(f32)
    tiny[1] = upper[6 * D :, :].astype(f32)
    quarters(mlp_in, x, y, mlp)
    quarters(attn_in, x, y, attn)
    for at in range(4):
        up_out[0, :, at * D : (at + 1) * D] = mlp[at].astype(f32)
        down_out[0, at * half : (at + 1) * half, :] = mlp[4 + at].astype(f32)
    q = half // 2
    for at in range(8):
        rows = slice((at % 2) * q, (at % 2 + 1) * q)
        value = attn[at, :q, :].astype(f32)
        if at < 6:
            qkv_out[0, rows, (at // 2) * D : (at // 2 + 1) * D] = value
        else:
            proj_out[0, rows, :] = value
    for at in range(2):
        tiny[0, at * 16 : (at + 1) * 16, :] = attn[at, q : q + 16, :].astype(f32)
    first = core == 0

    def own(row):
        return jnp.where(first, row[:, :half], row[:, half:])

    for layer in range(2):
        sums = tiny[layer]
        for norm in range(2):
            gains_out[layer, norm : norm + 1, :] = own(sums[8 * norm : 8 * norm + 1])
            shifts_out[layer, norm : norm + 1, :] = own(sums[8 * norm + 1 : 8 * norm + 2])
            qv_out[layer, norm : norm + 1, :] = own(sums[2 + norm : 3 + norm])
            up_b_out[layer : layer + 1, norm * D : (norm + 1) * D] = jnp.where(
                first, sums[11 + norm : 12 + norm], sums[13 + norm : 14 + norm]
            )
        proj_b_out[layer : layer + 1, :] = own(sums[4:5])
        down_b_out[layer : layer + 1, :] = own(sums[10:11])
        table_out[layer] = jnp.where(first, sums[16:24, :256], sums[24:32, :256])


def body(
    tokens,
    regions,
    rel_index,
    norm_gains,
    norm_shifts,
    qkv_weight,
    qv_bias,
    rel_table,
    proj_weight,
    proj_bias,
    fc1_weight,
    fc1_bias,
    fc2_weight,
    fc2_bias,
    cotangent,
):
    count = lax.axis_size("dp")
    images = tokens.shape[0]
    rows = images * CELL
    windows = images * 4
    own_small = jnp.concatenate(
        [
            norm_gains,
            norm_shifts,
            qv_bias,
            proj_bias[:, None],
            fc2_bias[:, None],
            fc1_bias.reshape(2, 4, D // 2),
        ],
        axis=1,
    )
    own_table = rel_table
    qkv_other = swap_cores(qkv_weight)
    proj_other = swap_cores(proj_weight)
    other_small = swap_cores(own_small)
    other_table = swap_cores(own_table)
    up_other = swap_cores(fc1_weight)
    down_other = swap_cores(fc2_weight)

    core = lax.axis_index("fsdp").astype(jnp.int32).reshape(1)
    eight = in_order(own_small[:, :8], other_small[:, :8], 2)
    four = in_order(
        own_small[:, 8:].reshape(2, 2, D), other_small[:, 8:].reshape(2, 2, D), 1
    )
    small_all = jnp.concatenate([eight, four, jnp.zeros((2, 4, D), bf16)], axis=1).astype(f32)
    table = in_order(own_table, other_table, 2)
    table = jnp.concatenate(
        [table, jnp.full((2, 1, HEADS), -1e30, bf16), jnp.zeros((2, LIVE - RELS - 1, HEADS), bf16)],
        axis=1,
    )
    grid_index = rel_index.reshape(WT, WT).T
    grid_index = jnp.pad(grid_index, ((0, 0), (0, ROWS - WT)))
    grid_index = jnp.pad(grid_index, ((0, ROWS - WT), (0, 0)), constant_values=RELS)
    onehot = (
        grid_index.reshape(1, ROWS * ROWS) == jnp.arange(LIVE, dtype=jnp.int32)[:, None]
    ).astype(bf16)
    bias_all = jnp.einsum("lrh,rp->lhp", table, onehot, preferred_element_type=f32)
    bias_all = (
        bias_all.reshape(2, QUADS, 4, ROWS, ROWS)
        .transpose(0, 1, 3, 2, 4)
        .reshape(2, QUADS, ROWS, 4 * ROWS)
    )
    region_win = (
        regions.reshape(2, WIN, 2, WIN).transpose(0, 2, 1, 3).reshape(4, WT)
    )
    mask = jnp.where(region_win[:, :, None] == region_win[:, None, :], 0.0, -100.0).astype(f32)
    mask = jnp.pad(mask, ((0, 0), (0, ROWS - WT), (0, ROWS - WT)))
    mask = jnp.tile(mask, (1, 1, 4))
    lay, unlay, to_moved, from_moved = [jnp.asarray(item, bf16) for item in permutations()]

    vmem = pltpu.VMEM
    wide = (rows, D)
    attn_w = [vmem((D, 3 * D), bf16), vmem((D, D), bf16)]
    mlp_w = [vmem((D, FF), bf16), vmem((FF, D), bf16)]
    two_sems = pltpu.SemaphoreType.DMA((2, 2))
    three_sems = pltpu.SemaphoreType.DMA((3, 2))
    attn_flops = 2 * rows * D * D * 5
    mlp_flops = 2 * rows * D * FF * 2
    current = tokens
    saved = []
    for layer in range(2):
        small = small_all[layer]
        middle, normed, qkv, probs, mixed = call(
            attention_forward_kernel,
            layer,
            rows,
            core,
            [
                current,
                lay,
                to_moved,
                from_moved,
                small,
                bias_all[layer],
                mask,
                qkv_weight,
                qkv_other,
                proj_weight,
                proj_other,
            ],
            "vvvvvvvaaaa",
            [
                shape(wide, f32),
                shape(wide, bf16),
                shape((rows, 3 * D), bf16),
                shape((windows, QUADS, ROWS, 4 * ROWS), f32),
                shape(wide, bf16),
            ],
            "vvvvv",
            attn_w + [vmem(wide if layer == 0 else (8, 128), f32), vmem(wide, bf16), two_sems],
            attn_flops,
        )
        result, normed_two, hidden, slope = call(
            mlp_forward_kernel,
            layer,
            rows,
            core,
            [middle, small, fc1_weight, up_other, fc2_weight, down_other],
            "vvaaaa",
            [
                shape(wide, f32),
                shape(wide, bf16),
                shape((rows, FF), bf16),
                shape((rows, FF), bf16),
            ],
            "vvvv",
            mlp_w + [two_sems],
            mlp_flops,
        )
        saved.append((current, middle, normed, qkv, probs, mixed, normed_two, hidden, slope, small))
        current = result
    at_dp = lax.axis_index("dp")
    bits = jnp.stack([at_dp & 1, (at_dp >> 1) & 1, lax.axis_index("fsdp")]).astype(jnp.int32)
    onehot_f = onehot.astype(f32)

    def small_rows(attn_sums, mlp_sums, pairs):
        flat = pairs.reshape(QUADS, ROWS, 4, ROWS).transpose(0, 2, 1, 3).reshape(HEADS, -1)
        heads = jnp.einsum("hp,rp->hr", flat, onehot_f, precision=lax.Precision.HIGHEST)
        heads = jnp.pad(heads, ((0, 0), (0, D - LIVE)))
        return jnp.concatenate([attn_sums, mlp_sums, heads], axis=0).astype(bf16)

    def backward(layer, grad, kept):
        source, middle, normed, qkv, probs, mixed, normed_two, hidden, slope, small = kept
        middle_grad, mlp_sums, mlp_keep, mlp_send = call(
            mlp_backward_kernel,
            layer,
            rows,
            core,
            [
                grad,
                lay,
                middle,
                normed_two,
                hidden,
                slope,
                small,
                fc1_weight,
                up_other,
                fc2_weight,
                down_other,
            ],
            "vvvvvvvaaaa",
            [
                shape(wide, f32),
                shape((8, D), f32),
                shape((FF, D), bf16),
                shape((FF, D), bf16),
            ],
            "vvaa",
            mlp_w
            + [
                vmem((2, FF, D), bf16),
                vmem((rows, FF), bf16),
                vmem(wide if layer == 1 else (8, 128), f32),
                vmem(wide, bf16),
                vmem((D, rows), bf16),
                vmem(wide, f32),
                three_sems,
            ],
            2 * mlp_flops,
        )
        mlp_got = swap_cores(mlp_send)
        if layer == 0:
            mlp_group = Group(2 * D, [
                (mlp_keep[: 2 * D], mlp_got[: 2 * D]),
                (mlp_keep[2 * D :], mlp_got[2 * D :]),
            ], count)
            mark = advance([mlp_group], bits, mlp_sums)
            middle_grad = after(mark, middle_grad)
        grad, attn_sums, pairs, attn_keep, attn_send = call(
            attention_backward_kernel,
            layer,
            rows,
            core,
            [
                middle_grad,
                source,
                lay,
                unlay,
                to_moved,
                from_moved,
                normed,
                qkv,
                probs,
                mixed,
                small,
                qkv_weight,
                qkv_other,
                proj_weight,
                proj_other,
            ],
            "vvvvvvvvvvvaaaa",
            [
                shape(wide if layer else (images, PIX, D), f32),
                shape((8, D), f32),
                shape((QUADS, ROWS, 4 * ROWS), f32),
                shape((2 * D, D), bf16),
                shape((2 * D, D), bf16),
            ],
            "vvvaa",
            attn_w
            + [
                vmem((2, 2 * D, D), bf16),
                vmem(wide if layer == 0 else (8, 128), f32),
                vmem(wide, bf16),
                vmem(wide, bf16),
                vmem((rows, 3 * D), bf16),
                vmem((rows, 3 * D) if layer else (16, 128), bf16),
                vmem((D, rows), bf16),
                vmem(wide, f32),
                three_sems,
            ],
            2 * attn_flops,
        )
        if layer == 0:
            held = (grad, attn_sums, pairs, attn_keep, attn_send, mlp_group.state)
            grad, attn_sums, pairs, attn_keep, attn_send, mlp_group.state = (
                lax.optimization_barrier(held)
            )
        attn_got = swap_cores(attn_send)
        tiny = small_rows(attn_sums, mlp_sums, pairs)
        tiny_got = swap_cores(tiny)
        if layer == 1:
            upper = pl.pallas_call(
                merge_kernel,
                out_shape=shape((6 * D + 32, D), bf16),
                compiler_params=pltpu.CompilerParams(vmem_limit_bytes=56 * 1024 * 1024),
                name="merge",
            )(mlp_keep, mlp_got, attn_keep, attn_got, tiny, tiny_got)
            return lax.optimization_barrier((upper, grad))
        pad = ((0, 96), (0, 0))
        attn_group = Group(
            D,
            [(attn_keep[:D], attn_got[:D]), (attn_keep[D:], attn_got[D:])],
            count,
            (jnp.pad(tiny, pad), jnp.pad(tiny_got, pad)),
        )
        groups = [mlp_group, attn_group]
        mark = grad
        while not all(group.done for group in groups):
            mark = advance([group for group in groups if not group.done], bits, mark)
        return [grad] + mlp_group.state + attn_group.state

    upper, grad = backward(1, cotangent, saved[1])
    upper = lax.psum(upper, "dp")
    taken = (grad, saved[0])
    grad, *arrived = lax.cond(
        lax.optimization_barrier(jnp.bool_(True)),
        lambda taken: backward(0, *taken),
        lambda taken: [
            jnp.zeros(item.shape, item.dtype)
            for item in jax.eval_shape(lambda taken: backward(0, *taken), taken)
        ],
        taken,
    )
    output = lax.reduce_precision(current, 8, 7).astype(bf16)
    output = (
        output.reshape(images, 2, 2, ROWS, D)[:, :, :, :WT]
        .reshape(images, 2, 2, WIN, WIN, D)
        .transpose(0, 1, 3, 2, 4, 5)
        .reshape(images, PIX, D)
    )
    pieces = [*arrived, upper]
    (
        qkv_g, proj_g, up_g, down_g, gains_g, shifts_g, qv_g, proj_b_g, up_b_g, down_b_g, heads,
    ) = pl.pallas_call(
        unpack_kernel,
        in_specs=[pl.BlockSpec(memory_space=pltpu.SMEM)]
        + [pl.BlockSpec(memory_space=pltpu.VMEM)] * len(pieces),
        out_specs=[pl.BlockSpec(memory_space=pltpu.VMEM)] * 11,
        out_shape=[
            shape(item.shape, f32)
            for item in (
                qkv_weight,
                proj_weight,
                fc1_weight,
                fc2_weight,
                norm_gains,
                norm_shifts,
                qv_bias,
                proj_bias,
                fc1_bias,
                fc2_bias,
            )
        ]
        + [shape((2, HEADS // 2, 256), f32)],
        scratch_shapes=[
            vmem((8, D // 2, D), bf16),
            vmem((8, D // 4 + 16, D), bf16),
            vmem((2, 32, D), f32),
        ],
        compiler_params=pltpu.CompilerParams(vmem_limit_bytes=56 * 1024 * 1024),
        name="unpack",
    )(bits, *pieces)
    table_g = heads[:, :, :RELS].transpose(0, 2, 1)
    return (
        output,
        grad,
        gains_g,
        shifts_g,
        qkv_g,
        qv_g,
        table_g,
        proj_g,
        proj_b_g,
        up_g,
        up_b_g,
        down_g,
        down_b_g,
    )


def solution(mesh):
    return jax.shard_map(
        body,
        mesh=mesh,
        in_specs=(
            P(("dp", "fsdp"), None, None),
            P(),
            P(),
            P(None, None, "fsdp"),
            P(None, None, "fsdp"),
            P(None, "fsdp", None),
            P(None, None, "fsdp"),
            P(None, None, "fsdp"),
            P(None, "fsdp", None),
            P(None, "fsdp"),
            P(None, "fsdp", None),
            P(None, "fsdp"),
            P(None, "fsdp", None),
            P(None, "fsdp"),
            P(("dp", "fsdp"), None, None),
        ),
        out_specs=(
            P(("dp", "fsdp"), None, None),
            P(("dp", "fsdp"), None, None),
            P(None, None, "fsdp"),
            P(None, None, "fsdp"),
            P(None, "fsdp", None),
            P(None, None, "fsdp"),
            P(None, None, "fsdp"),
            P(None, "fsdp", None),
            P(None, "fsdp"),
            P(None, "fsdp", None),
            P(None, "fsdp"),
            P(None, "fsdp", None),
            P(None, "fsdp"),
        ),
        check_vma=False,
    )
```

```python
import functools

import numpy as np

import jax
import jax.numpy as jnp
from jax import lax
from jax.experimental import pallas as pl
from jax.experimental.pallas import tpu as pltpu
from jax.sharding import PartitionSpec as P

D = 512
HEADS = 16
HD = 32
FF = 2048
WIN = 7
IMG = 14
SHIFT = 3
PIX = 196
WT = 49
RELS = 169
ROWS = 64
CELL = 256
QUADS = 4
TIE = 0
LIVE = 176

norm_eps = 1e-05
scale = HD**-0.5
f32 = jnp.float32
bf16 = jnp.bfloat16


def place(offset):
    rows = np.full((CELL,), -1, np.int64)
    for i in range(IMG):
        for j in range(IMG):
            window = (i // WIN) * 2 + j // WIN
            row = window * ROWS + (i % WIN) * WIN + j % WIN
            rows[row] = ((i + offset) % IMG) * IMG + (j + offset) % IMG
    return rows


def permutations():
    base, moved = place(0), place(SHIFT)
    lay = np.zeros((CELL, PIX), np.float32)
    lay[base >= 0, base[base >= 0]] = 1
    shifted = np.zeros((CELL, PIX), np.float32)
    shifted[moved >= 0, moved[moved >= 0]] = 1
    return lay, lay.T.copy(), shifted @ lay.T, lay @ shifted.T


def dot(a, b):
    return jnp.dot(a, b, preferred_element_type=f32)


def dot_nt(a, b):
    return lax.dot_general(a, b, (((1,), (1,)), ((), ())), preferred_element_type=f32)


def dot_tn(a, b):
    return lax.dot_general(a, b, (((0,), (0,)), ((), ())), preferred_element_type=f32)


def loop(count, step):
    def run(at, carry):
        step(at)
        return carry

    lax.fori_loop(0, count, run, 0)


def span(at, size):
    return pl.ds(pl.multiple_of(at * size, size), size)


def normal(values):
    centred = values - jnp.mean(values, -1, keepdims=True)
    spread = lax.rsqrt(jnp.mean(centred * centred, -1, keepdims=True) + norm_eps)
    return centred * spread, spread


def norm_rows(source, target, gain, shift, rows):
    def step(at):
        part = span(at, 128)
        unit, _ = normal(source[part, :])
        target[part, :] = (unit * gain + shift).astype(bf16)

    loop(rows // 128, step)


def norm_back(grad, source, gain, extra, target, rows):
    def step(at, sums):
        part = span(at, 128)
        dh = grad[part, :]
        unit, spread = normal(source[part, :])
        du = dh * gain
        back = spread * (
            du
            - jnp.mean(du, -1, keepdims=True)
            - unit * jnp.mean(du * unit, -1, keepdims=True)
        )
        target[part, :] = extra[part, :] + back
        return (
            sums[0] + jnp.sum(dh * unit, 0, keepdims=True),
            sums[1] + jnp.sum(dh, 0, keepdims=True),
        )

    zero = jnp.zeros((1, D), f32)
    return lax.fori_loop(0, rows // 128, step, (zero, zero))


def move(matrix, source, target, rows, columns):
    for image in range(rows // CELL):
        for at in range(columns // D):
            target[image * CELL : (image + 1) * CELL, at * D : (at + 1) * D] = dot(
                matrix, source[image * CELL : (image + 1) * CELL, at * D : (at + 1) * D]
            ).astype(bf16)


def fetch(core, layer, own, other, target, sems):
    half = own.shape[1]
    mine = pltpu.make_async_copy(
        own.at[layer], target.at[pl.ds(pl.multiple_of(core * half, half), half), :], sems.at[0]
    )
    theirs = pltpu.make_async_copy(
        other.at[layer],
        target.at[pl.ds(pl.multiple_of((1 - core) * half, half), half), :],
        sems.at[1],
    )
    mine.start()
    theirs.start()

    def wait():
        mine.wait()
        theirs.wait()

    return wait


def give(core, grads, keep, send, sems):
    one = pltpu.make_async_copy(grads.at[core], keep, sems.at[0])
    two = pltpu.make_async_copy(grads.at[1 - core], send, sems.at[1])
    one.start()
    two.start()
    one.wait()
    two.wait()


def head_masks():
    lanes = lax.broadcasted_iota(jnp.int32, (ROWS, 128), 1) // HD
    return [lanes == at for at in range(QUADS)]


def stack_heads(value, masks):
    zero = jnp.zeros_like(value)
    return jnp.concatenate([jnp.where(mask, value, zero) for mask in masks], axis=0)


def pick_heads(value, masks):
    result = value[:ROWS]
    for at in range(1, QUADS):
        result = jnp.where(masks[at], value[at * ROWS : (at + 1) * ROWS], result)
    return result


def attention_forward_kernel(
    layer,
    rows,
    core_ref,
    source,
    lay,
    to_moved,
    from_moved,
    small,
    bias,
    mask,
    qkv_own,
    qkv_other,
    proj_own,
    proj_other,
    middle,
    normed,
    qkv,
    probs,
    mixed,
    qkv_w,
    proj_w,
    tokens_in,
    work,
    sems,
):
    core = core_ref[0]
    wait_qkv = fetch(core, layer, qkv_own, qkv_other, qkv_w, sems.at[0])
    wait_proj = fetch(core, layer, proj_own, proj_other, proj_w, sems.at[1])
    if layer == 0:
        for image in range(rows // CELL):
            tokens_in[image * CELL : (image + 1) * CELL, :] = dot(lay[...], source[image])
    else:
        tokens_in = source
    norm_rows(tokens_in, normed, small[0:1, :], small[2:3, :], rows)
    if layer == 0:
        moved = normed
    else:
        move(to_moved[...], normed, work, rows, D)
        moved = work
    wait_qkv()
    for at in range(3):
        part = dot(moved[...], qkv_w[:, at * D : (at + 1) * D])
        if at == 0:
            part = part + small[4:5, :]
        if at == 2:
            part = part + small[5:6, :]
        qkv[:, at * D : (at + 1) * D] = part.astype(bf16)
    masks = head_masks()
    out = mixed if layer == 0 else work

    def window(at):
        part = span(at, ROWS)
        for quad in range(QUADS):
            lanes = slice(quad * 128, (quad + 1) * 128)
            queries = stack_heads(qkv[part, lanes], masks)
            keys = qkv[part, D + quad * 128 : D + (quad + 1) * 128]
            values = qkv[part, 2 * D + quad * 128 : 2 * D + (quad + 1) * 128]
            scores = scale * dot_nt(keys, queries) + bias[layer, quad]
            if layer:
                scores = scores + mask[at % 4]
            expo = jnp.exp(scores - jnp.max(scores, 0, keepdims=True))
            prob = expo / jnp.sum(expo, 0, keepdims=True)
            probs[at, quad] = prob
            mix = dot_tn(prob.astype(bf16), values)
            out[part, lanes] = pick_heads(mix, masks).astype(bf16)

    loop(rows // ROWS, window)
    if layer:
        move(from_moved[...], work, mixed, rows, D)
    wait_proj()
    middle[...] = tokens_in[...] + dot(mixed[...], proj_w[...]) + small[6:7, :]


def mlp_forward_kernel(
    layer,
    rows,
    core_ref,
    middle,
    small,
    up_own,
    up_other,
    down_own,
    down_other,
    result,
    normed,
    hidden,
    slope,
    up_w,
    down_w,
    sems,
):
    core = core_ref[0]
    wait_up = fetch(core, layer, up_own, up_other, up_w, sems.at[0])
    wait_down = fetch(core, layer, down_own, down_other, down_w, sems.at[1])
    norm_rows(middle, normed, small[1:2, :], small[3:4, :], rows)
    wait_up()

    def step(at):
        part = span(at, 256)
        inner = dot(normed[...], up_w[:, part])
        row = 8 + at // 2
        inner = inner + small[pl.ds(row, 1), span(at % 2, 256)]
        below = 0.5 * (1.0 + lax.erf(inner * (0.5**0.5)))
        hidden[:, part] = (inner * below).astype(bf16)
        slope[:, part] = (
            below + inner * (jnp.exp(-0.5 * inner * inner) * ((2 * np.pi) ** -0.5))
        ).astype(bf16)

    loop(FF // 256, step)
    wait_down()
    result[...] = (
        middle[...] + dot(hidden[...], down_w[...]) + small[7:8, :]
    ).astype(result.dtype)


def mlp_backward_kernel(
    layer,
    rows,
    core_ref,
    grad,
    lay,
    middle,
    normed,
    hidden,
    slope,
    small,
    up_own,
    up_other,
    down_own,
    down_other,
    middle_grad,
    sums,
    keep,
    send,
    up_w,
    down_w,
    grads,
    inner_grad,
    grad_in,
    low,
    turned,
    normed_grad,
    sems,
):
    core = core_ref[0]
    wait_up = fetch(core, layer, up_own, up_other, up_w, sems.at[0])
    wait_down = fetch(core, layer, down_own, down_other, down_w, sems.at[1])
    if layer == 1:
        for image in range(rows // CELL):
            grad_in[image * CELL : (image + 1) * CELL, :] = dot(lay[...], grad[image])
    else:
        grad_in = grad
    low[...] = grad_in[...].astype(bf16)
    sums[...] = jnp.zeros(sums.shape, f32)
    sums[2:3, :] = jnp.sum(low[...].astype(f32), 0, keepdims=True)
    turned[...] = normed[...].T
    wait_down()

    def step(at):
        part = span(at, 256)
        back = dot_nt(low[...], down_w[part, :]) * slope[:, part].astype(f32)
        back = back.astype(bf16)
        inner_grad[:, part] = back
        sums[pl.ds(3 + at // 2, 1), span(at % 2, 256)] = jnp.sum(
            back.astype(f32), 0, keepdims=True
        )
        down_grad = dot(hidden[:, part].T, low[...]).astype(bf16)
        grads[at // 4, pl.ds(pl.multiple_of(1024 + (at % 4) * 256, 256), 256), :] = down_grad
        up_grad = dot(turned[...], back).astype(bf16)
        place_at = pl.ds(pl.multiple_of((at // 2) * 256, 256), 256)
        lanes = span(at % 2, 256)
        grads[0, place_at, lanes] = up_grad[:256]
        grads[1, place_at, lanes] = up_grad[256:]

    loop(FF // 256, step)
    wait_up()
    normed_grad[...] = dot_nt(inner_grad[...], up_w[...])
    gain_sum, shift_sum = norm_back(normed_grad, middle, small[1:2, :], grad_in, middle_grad, rows)
    sums[0:1, :] = gain_sum
    sums[1:2, :] = shift_sum
    give(core, grads, keep, send, sems.at[2])


def attention_backward_kernel(
    layer,
    rows,
    core_ref,
    middle_grad,
    source,
    lay,
    unlay,
    to_moved,
    from_moved,
    normed,
    qkv,
    probs,
    mixed,
    small,
    qkv_own,
    qkv_other,
    proj_own,
    proj_other,
    source_grad,
    sums,
    pairs,
    keep,
    send,
    qkv_w,
    proj_w,
    grads,
    tokens_in,
    low,
    mix_grad,
    joined,
    moved_grad,
    turned,
    normed_grad,
    sems,
):
    core = core_ref[0]
    wait_qkv = fetch(core, layer, qkv_own, qkv_other, qkv_w, sems.at[0])
    wait_proj = fetch(core, layer, proj_own, proj_other, proj_w, sems.at[1])
    if layer == 0:
        for image in range(rows // CELL):
            tokens_in[image * CELL : (image + 1) * CELL, :] = dot(lay[...], source[image])
    else:
        tokens_in = source
    low[...] = middle_grad[...].astype(bf16)
    sums[...] = jnp.zeros(sums.shape, f32)
    sums[4:5, :] = jnp.sum(low[...].astype(f32), 0, keepdims=True)
    turned[...] = mixed[...].T
    for side in range(2):
        grads[side, 768:1024, :] = dot(turned[side * 256 : (side + 1) * 256, :], low[...]).astype(
            bf16
        )
    wait_proj()
    if layer == 0:
        mix_grad[...] = dot_nt(low[...], proj_w[...]).astype(bf16)
        target = joined
    else:
        moved_grad[:, :D] = dot_nt(low[...], proj_w[...]).astype(bf16)
        move(to_moved[...], moved_grad, mix_grad, rows, D)
        target = moved_grad
    pairs[...] = jnp.zeros(pairs.shape, f32)
    masks = head_masks()

    def window(at):
        part = span(at, ROWS)
        for quad in range(QUADS):
            queries = stack_heads(qkv[part, quad * 128 : (quad + 1) * 128], masks)
            keys = qkv[part, D + quad * 128 : D + (quad + 1) * 128]
            values = qkv[part, 2 * D + quad * 128 : 2 * D + (quad + 1) * 128]
            given = stack_heads(mix_grad[part, quad * 128 : (quad + 1) * 128], masks)
            prob = probs[at, quad]
            prob_grad = dot_nt(values, given)
            delta = jnp.sum(prob_grad * prob, 0, keepdims=True)
            score_grad = (prob * (prob_grad - delta)).astype(bf16)
            pairs[quad] += score_grad.astype(f32)
            values_grad = dot(prob.astype(bf16), given)
            keys_grad = scale * dot(score_grad, queries)
            queries_grad = scale * pick_heads(dot_tn(score_grad, keys), masks)
            target[part, quad * 128 : (quad + 1) * 128] = queries_grad.astype(bf16)
            target[part, D + quad * 128 : D + (quad + 1) * 128] = keys_grad.astype(bf16)
            target[part, 2 * D + quad * 128 : 2 * D + (quad + 1) * 128] = values_grad.astype(bf16)

    loop(rows // ROWS, window)
    if layer:
        move(from_moved[...], moved_grad, joined, rows, 3 * D)
    sums[2:3, :] = jnp.sum(joined[:, :D].astype(f32), 0, keepdims=True)
    sums[3:4, :] = jnp.sum(joined[:, 2 * D :].astype(f32), 0, keepdims=True)
    turned[...] = normed[...].T
    for at in range(3):
        for side in range(2):
            grads[side, at * 256 : (at + 1) * 256, :] = dot(
                turned[side * 256 : (side + 1) * 256, :], joined[:, at * D : (at + 1) * D]
            ).astype(bf16)
    wait_qkv()
    normed_grad[...] = dot_nt(joined[...], qkv_w[...])
    if layer == 0:
        gain_sum, shift_sum = norm_back(
            normed_grad, tokens_in, small[0:1, :], middle_grad, normed_grad, rows
        )
        for image in range(rows // CELL):
            value = normed_grad[image * CELL : (image + 1) * CELL, :]
            high = value.astype(bf16)
            rest = value - high.astype(f32)
            fine = rest.astype(bf16)
            last = (rest - fine.astype(f32)).astype(bf16)
            source_grad[image] = (
                dot(unlay[...], high) + dot(unlay[...], fine) + dot(unlay[...], last)
            )
    else:
        gain_sum, shift_sum = norm_back(
            normed_grad, tokens_in, small[0:1, :], middle_grad, source_grad, rows
        )
    sums[0:1, :] = gain_sum
    sums[1:2, :] = shift_sum
    give(core, grads, keep, send, sems.at[2])


def call(kernel, layer, rows, core, inputs, kinds, outs, out_kinds, scratch, flops):
    spaces = {"v": pltpu.VMEM, "a": pl.ANY}
    return pl.pallas_call(
        functools.partial(kernel, layer, rows),
        in_specs=[pl.BlockSpec(memory_space=pltpu.SMEM)]
        + [pl.BlockSpec(memory_space=spaces[kind]) for kind in kinds],
        out_specs=[pl.BlockSpec(memory_space=spaces[kind]) for kind in out_kinds],
        out_shape=outs,
        scratch_shapes=scratch,
        compiler_params=pltpu.CompilerParams(vmem_limit_bytes=30 * 1024 * 1024),
        cost_estimate=pl.CostEstimate(flops=1, bytes_accessed=1, transcendentals=0),
        name=kernel.__name__ + str(layer),
    )(core, *inputs)


def shape(dims, dtype):
    return jax.ShapeDtypeStruct(dims, dtype)


def swap_cores(value):
    return lax.ppermute(value, "fsdp", [(0, 1), (1, 0)])


def in_order(own, other, axis):
    first = lax.axis_index("fsdp") == 0
    return jnp.concatenate([jnp.where(first, own, other), jnp.where(first, other, own)], axis=axis)


def dp_swap(value, bit, count):
    return lax.ppermute(value, "dp", [(at, at ^ (1 << bit)) for at in range(count)])


def plus(one, two):
    return (one.astype(f32) + two.astype(f32)).astype(bf16)


def op_first(bits, ins, outs):
    quarter = outs[0].shape[0] // 2
    for part in range(2):
        keep, got = ins[2 * part : 2 * part + 2]
        send, hold = outs[2 * part : 2 * part + 2]
        side = bits[part]
        for low in range(2):
            rows = slice(low * quarter, (low + 1) * quarter)
            send[rows, :] = plus(keep[2 * (1 - side) + low], got[2 * (1 - side) + low])
            hold[rows, :] = plus(keep[2 * side + low], got[2 * side + low])


def op_first_small(bits, ins, outs):
    quarter = outs[0].shape[0] // 2
    rows_in = quarter - 16
    tiny, tiny_got = ins[4:6]
    for part in range(2):
        keep, got = ins[2 * part : 2 * part + 2]
        send, hold = outs[2 * part : 2 * part + 2]
        side = bits[part]
        for low in range(2):
            first = slice(low * quarter, low * quarter + rows_in)
            last = slice(low * quarter + rows_in, (low + 1) * quarter)
            for target, at in ((send, 2 * (1 - side) + low), (hold, 2 * side + low)):
                target[first, :] = plus(keep[at], got[at])
                target[last, :] = plus(tiny[4 * part + at], tiny_got[4 * part + at])


def op_second(bits, ins, outs):
    for part in range(2):
        hold, got = ins[2 * part : 2 * part + 2]
        send, rest = outs[2 * part : 2 * part + 2]
        side = bits[1 - part]
        send[...] = plus(hold[1 - side], got[1 - side])
        rest[...] = plus(hold[side], got[side])


def op_join(bits, ins, outs):
    quarter = ins[0].shape[0]
    for part in range(2):
        outs[0][part * quarter : (part + 1) * quarter, :] = plus(
            ins[2 * part][...], ins[2 * part + 1][...]
        )


def op_add(bits, ins, outs):
    outs[0][...] = plus(ins[0][...], ins[1][...])


def step_kernel(plan, bits_ref, *refs):
    bits = (bits_ref[0], bits_ref[1])
    total = sum(item[1] for item in plan)
    ins, outs = refs[:total], refs[total:]
    for op, inputs, outputs in plan:
        op(bits, ins[:inputs], outs[:outputs])
        ins, outs = ins[inputs:], outs[outputs:]


class Group:
    def __init__(self, rows, parts, count, tiny=None):
        self.small = tiny
        self.quarter = rows // 4 + (16 if tiny else 0)
        self.parts = parts
        self.count = count
        self.stage = 0
        self.later = count.bit_length() - 3
        self.done = False

    def low(self, rows):
        return shape((rows, D), bf16)

    def next_op(self):
        q = self.quarter
        if self.stage == 0:
            ins = [item.reshape(4, -1, D) for pair in self.parts for item in pair]
            if self.small:
                ins += [item.reshape(8, 16, D) for item in self.small]
            return op_first_small if self.small else op_first, ins, [self.low(2 * q)] * 4
        if self.stage == 1:
            ins = [item.reshape(2, q, D) for item in self.state]
            return op_second, ins, [self.low(q)] * 4
        if self.stage == 2:
            return op_join, self.state, [self.low(2 * q)]
        if self.stage < 3 + self.later:
            return op_add, self.state, [self.low(2 * q)]
        return None

    def send(self, outs):
        if self.stage < 2:
            first, second = (0, 1) if self.stage == 0 else (1, 0)
            self.state = [
                outs[1],
                dp_swap(outs[0], first, self.count),
                outs[3],
                dp_swap(outs[2], second, self.count),
            ]
        elif self.stage < 2 + self.later:
            self.state = [outs[0], dp_swap(outs[0], self.stage, self.count)]
        elif self.stage == 2 + self.later:
            mine = outs[0]
            self.state = [mine, dp_swap(mine, 0, self.count), dp_swap(mine, 1, self.count)]
        else:
            q = self.quarter
            mine, by_x, by_y = self.state
            self.state = [
                mine,
                by_x,
                by_y,
                dp_swap(by_x[:q], 1, self.count),
                dp_swap(by_y[q:], 0, self.count),
            ]
            self.done = True
        self.stage += 1


def after(first, then):
    return lax.optimization_barrier((first, then))[1]


def advance(groups, bits, when, final=False):
    ops, marks = [], []
    for group in groups:
        op = group.next_op()
        if op is None:
            group.state = list(after(when, group.state))
            group.send(None)
        else:
            ops.append((group, op))
    if not ops:
        return when
    plan = tuple((op[0], len(op[1]), len(op[2])) for _, op in ops)
    inputs = [item for _, op in ops for item in op[1]]
    outs = [item for _, op in ops for item in op[2]]
    inputs = after(when, inputs)
    results = pl.pallas_call(
        functools.partial(step_kernel, plan),
        in_specs=[pl.BlockSpec(memory_space=pltpu.SMEM)]
        + [pl.BlockSpec(memory_space=pltpu.VMEM)] * len(inputs),
        out_specs=[pl.BlockSpec(memory_space=pltpu.VMEM)] * len(outs),
        out_shape=outs,
        compiler_params=pltpu.CompilerParams(vmem_limit_bytes=30 * 1024 * 1024),
        cost_estimate=pl.CostEstimate(flops=1, bytes_accessed=1, transcendentals=0),
        name="reduce_step",
    )(bits, *inputs)
    for group, op in ops:
        mine, results = results[: len(op[2])], results[len(op[2]) :]
        group.send(mine)
        marks.append(mine[0])
    return marks[0]


def merge_kernel(*refs):
    out = refs[-1]
    start = 0
    for at in range(0, len(refs) - 1, 2):
        rows = refs[at].shape[0]
        out[start : start + rows, :] = plus(refs[at][...], refs[at + 1][...])
        start += rows


def quarters(ins, x, y, target):
    mine, by_x, by_y, far_first, far_second = ins
    q = far_first.shape[0]
    target[x * 2 + y] = mine[:q, :]
    target[(1 - x) * 2 + y] = by_x[:q, :]
    target[x * 2 + 1 - y] = by_y[:q, :]
    target[(1 - x) * 2 + 1 - y] = far_first[...]
    target[4 + y * 2 + x] = mine[q:, :]
    target[4 + y * 2 + 1 - x] = by_x[q:, :]
    target[4 + (1 - y) * 2 + x] = by_y[q:, :]
    target[4 + (1 - y) * 2 + 1 - x] = far_second[...]


def unpack_kernel(bits_ref, *refs):
    x, y, core = bits_ref[0], bits_ref[1], bits_ref[2]
    mlp_in, attn_in, upper = refs[:5], refs[5:10], refs[10]
    qkv_out, proj_out, up_out, down_out = refs[11:15]
    gains_out, shifts_out, qv_out, proj_b_out, up_b_out, down_b_out, table_out = refs[15:22]
    mlp, attn, tiny = refs[22:]
    half = D // 2
    for at in range(2):
        up_out[1, :, 2 * at * D : (2 * at + 1) * D] = upper[2 * at * half : (2 * at + 1) * half, :].astype(f32)
        up_out[1, :, (2 * at + 1) * D : (2 * at + 2) * D] = upper[
            (2 * at + 1) * half : (2 * at + 2) * half, :
        ].astype(f32)
    down_out[1] = upper[2 * D : 4 * D, :].astype(f32)
    for at in range(3):
        qkv_out[1, :, at * D : (at + 1) * D] = upper[
            4 * D + at * half : 4 * D + (at + 1) * half, :
        ].astype(f32)
    proj_out[1] = upper[4 * D + 3 * half : 6 * D, :].astype(f32)
    tiny[1, :16, :] = upper[6 * D :, :].astype(f32)
    quarters(mlp_in, x, y, mlp)
    quarters(attn_in, x, y, attn)
    for at in range(4):
        up_out[0, :, at * D : (at + 1) * D] = mlp[at].astype(f32)
        down_out[0, at * half : (at + 1) * half, :] = mlp[4 + at].astype(f32)
    q = half // 2
    for at in range(8):
        rows = slice((at % 2) * q, (at % 2 + 1) * q)
        value = attn[at, :q, :].astype(f32)
        if at < 6:
            qkv_out[0, rows, (at // 2) * D : (at // 2 + 1) * D] = value
        else:
            proj_out[0, rows, :] = value
    for at in range(2):
        tiny[0, at * 16 : (at + 1) * 16, :] = attn[at, q : q + 16, :].astype(f32)
    tiny[1, 16:, :] = attn[2, q : q + 16, :].astype(f32)
    first = core == 0

    def own(row):
        return jnp.where(first, row[:, :half], row[:, half:])

    for layer in range(2):
        sums = tiny[layer]
        for norm in range(2):
            gains_out[layer, norm : norm + 1, :] = own(sums[8 * norm : 8 * norm + 1])
            shifts_out[layer, norm : norm + 1, :] = own(sums[8 * norm + 1 : 8 * norm + 2])
            qv_out[layer, norm : norm + 1, :] = own(sums[2 + norm : 3 + norm])
            up_b_out[layer : layer + 1, norm * D : (norm + 1) * D] = jnp.where(
                first, sums[11 + norm : 12 + norm], sums[13 + norm : 14 + norm]
            )
        proj_b_out[layer : layer + 1, :] = own(sums[4:5])
        down_b_out[layer : layer + 1, :] = own(sums[10:11])
        table_out[layer] = jnp.where(first, sums[16:24, :256], sums[24:32, :256])


def body(
    tokens,
    regions,
    rel_index,
    norm_gains,
    norm_shifts,
    qkv_weight,
    qv_bias,
    rel_table,
    proj_weight,
    proj_bias,
    fc1_weight,
    fc1_bias,
    fc2_weight,
    fc2_bias,
    cotangent,
):
    count = lax.axis_size("dp")
    images = tokens.shape[0]
    rows = images * CELL
    windows = images * 4
    own_small = jnp.concatenate(
        [
            norm_gains,
            norm_shifts,
            qv_bias,
            proj_bias[:, None],
            fc2_bias[:, None],
            fc1_bias.reshape(2, 4, D // 2),
        ],
        axis=1,
    )
    own_table = rel_table
    qkv_other = swap_cores(qkv_weight)
    proj_other = swap_cores(proj_weight)
    other_small = swap_cores(own_small)
    other_table = swap_cores(own_table)
    up_other = swap_cores(fc1_weight)
    down_other = swap_cores(fc2_weight)

    core = lax.axis_index("fsdp").astype(jnp.int32).reshape(1)
    eight = in_order(own_small[:, :8], other_small[:, :8], 2)
    four = in_order(
        own_small[:, 8:].reshape(2, 2, D), other_small[:, 8:].reshape(2, 2, D), 1
    )
    small_all = jnp.concatenate([eight, four, jnp.zeros((2, 4, D), bf16)], axis=1).astype(f32)
    table = in_order(own_table, other_table, 2)
    table = jnp.concatenate(
        [table, jnp.full((2, 1, HEADS), -1e30, bf16), jnp.zeros((2, LIVE - RELS - 1, HEADS), bf16)],
        axis=1,
    )
    grid_index = rel_index.reshape(WT, WT).T
    grid_index = jnp.pad(grid_index, ((0, 0), (0, ROWS - WT)))
    grid_index = jnp.pad(grid_index, ((0, ROWS - WT), (0, 0)), constant_values=RELS)
    onehot = (
        grid_index.reshape(1, ROWS * ROWS) == jnp.arange(LIVE, dtype=jnp.int32)[:, None]
    ).astype(bf16)
    bias_all = jnp.einsum("lrh,rp->lhp", table, onehot, preferred_element_type=f32)
    bias_all = (
        bias_all.reshape(2, QUADS, 4, ROWS, ROWS)
        .transpose(0, 1, 3, 2, 4)
        .reshape(2, QUADS, ROWS, 4 * ROWS)
    )
    region_win = (
        regions.reshape(2, WIN, 2, WIN).transpose(0, 2, 1, 3).reshape(4, WT)
    )
    mask = jnp.where(region_win[:, :, None] == region_win[:, None, :], 0.0, -100.0).astype(f32)
    mask = jnp.pad(mask, ((0, 0), (0, ROWS - WT), (0, ROWS - WT)))
    mask = jnp.tile(mask, (1, 1, 4))
    lay, unlay, to_moved, from_moved = [jnp.asarray(item, bf16) for item in permutations()]

    vmem = pltpu.VMEM
    wide = (rows, D)
    attn_w = [vmem((D, 3 * D), bf16), vmem((D, D), bf16)]
    mlp_w = [vmem((D, FF), bf16), vmem((FF, D), bf16)]
    two_sems = pltpu.SemaphoreType.DMA((2, 2))
    three_sems = pltpu.SemaphoreType.DMA((3, 2))
    attn_flops = 2 * rows * D * D * 5
    mlp_flops = 2 * rows * D * FF * 2
    current = tokens
    saved = []
    for layer in range(2):
        small = small_all[layer]
        middle, normed, qkv, probs, mixed = call(
            attention_forward_kernel,
            layer,
            rows,
            core,
            [
                current,
                lay,
                to_moved,
                from_moved,
                small,
                bias_all,
                mask,
                qkv_weight,
                qkv_other,
                proj_weight,
                proj_other,
            ],
            "vvvvvvvaaaa",
            [
                shape(wide, f32),
                shape(wide, bf16),
                shape((rows, 3 * D), bf16),
                shape((windows, QUADS, ROWS, 4 * ROWS), f32),
                shape(wide, bf16),
            ],
            "vvvvv",
            attn_w + [vmem(wide if layer == 0 else (8, 128), f32), vmem(wide, bf16), two_sems],
            attn_flops,
        )
        result, normed_two, hidden, slope = call(
            mlp_forward_kernel,
            layer,
            rows,
            core,
            [middle, small, fc1_weight, up_other, fc2_weight, down_other],
            "vvaaaa",
            [
                shape(wide, f32),
                shape(wide, bf16),
                shape((rows, FF), bf16),
                shape((rows, FF), bf16),
            ],
            "vvvv",
            mlp_w + [two_sems],
            mlp_flops,
        )
        saved.append((current, middle, normed, qkv, probs, mixed, normed_two, hidden, slope, small))
        current = result
    at_dp = lax.axis_index("dp")
    bits = jnp.stack([at_dp & 1, (at_dp >> 1) & 1, lax.axis_index("fsdp")]).astype(jnp.int32)
    onehot_f = onehot.astype(f32)

    def table_rows(pairs):
        flat = (
            pairs.reshape(2, QUADS, ROWS, 4, ROWS).transpose(0, 1, 3, 2, 4).reshape(2 * HEADS, -1)
        )
        heads = jnp.einsum("hp,rp->hr", flat, onehot_f, precision=lax.Precision.HIGH)
        return jnp.pad(heads, ((0, 0), (0, D - LIVE)))

    def backward(layer, grad, kept, pairs_upper=None):
        source, middle, normed, qkv, probs, mixed, normed_two, hidden, slope, small = kept
        middle_grad, mlp_sums, mlp_keep, mlp_send = call(
            mlp_backward_kernel,
            layer,
            rows,
            core,
            [
                grad,
                lay,
                middle,
                normed_two,
                hidden,
                slope,
                small,
                fc1_weight,
                up_other,
                fc2_weight,
                down_other,
            ],
            "vvvvvvvaaaa",
            [
                shape(wide, f32),
                shape((8, D), f32),
                shape((FF, D), bf16),
                shape((FF, D), bf16),
            ],
            "vvaa",
            mlp_w
            + [
                vmem((2, FF, D), bf16),
                vmem((rows, FF), bf16),
                vmem(wide if layer == 1 else (8, 128), f32),
                vmem(wide, bf16),
                vmem((D, rows), bf16),
                vmem(wide, f32),
                three_sems,
            ],
            2 * mlp_flops,
        )
        mlp_got = swap_cores(mlp_send)
        if layer == 0:
            mlp_group = Group(2 * D, [
                (mlp_keep[: 2 * D], mlp_got[: 2 * D]),
                (mlp_keep[2 * D :], mlp_got[2 * D :]),
            ], count)
            mark = advance([mlp_group], bits, mlp_sums)
            middle_grad = after(mark, middle_grad)
        grad, attn_sums, pairs, attn_keep, attn_send = call(
            attention_backward_kernel,
            layer,
            rows,
            core,
            [
                middle_grad,
                source,
                lay,
                unlay,
                to_moved,
                from_moved,
                normed,
                qkv,
                probs,
                mixed,
                small,
                qkv_weight,
                qkv_other,
                proj_weight,
                proj_other,
            ],
            "vvvvvvvvvvvaaaa",
            [
                shape(wide if layer else (images, PIX, D), f32),
                shape((8, D), f32),
                shape((QUADS, ROWS, 4 * ROWS), f32),
                shape((2 * D, D), bf16),
                shape((2 * D, D), bf16),
            ],
            "vvvaa",
            attn_w
            + [
                vmem((2, 2 * D, D), bf16),
                vmem(wide if layer == 0 else (8, 128), f32),
                vmem(wide, bf16),
                vmem(wide, bf16),
                vmem((rows, 3 * D), bf16),
                vmem((rows, 3 * D) if layer else (16, 128), bf16),
                vmem((D, rows), bf16),
                vmem(wide, f32),
                three_sems,
            ],
            2 * attn_flops,
        )
        if layer == 0:
            held = (grad, attn_sums, pairs, attn_keep, attn_send, mlp_group.state)
            grad, attn_sums, pairs, attn_keep, attn_send, mlp_group.state = (
                lax.optimization_barrier(held)
            )
        attn_got = swap_cores(attn_send)
        tiny = [attn_sums, mlp_sums]
        if layer == 0:
            tiny.append(table_rows(jnp.stack([pairs, pairs_upper])))
        tiny = jnp.concatenate(tiny, axis=0).astype(bf16)
        tiny_got = swap_cores(tiny)
        if layer == 1:
            upper = pl.pallas_call(
                merge_kernel,
                out_shape=shape((6 * D + 16, D), bf16),
                compiler_params=pltpu.CompilerParams(vmem_limit_bytes=30 * 1024 * 1024),
                name="merge",
            )(mlp_keep, mlp_got, attn_keep, attn_got, tiny, tiny_got)
            return lax.optimization_barrier((upper, grad, pairs))
        pad = ((0, 80), (0, 0))
        attn_group = Group(
            D,
            [(attn_keep[:D], attn_got[:D]), (attn_keep[D:], attn_got[D:])],
            count,
            (jnp.pad(tiny, pad), jnp.pad(tiny_got, pad)),
        )
        groups = [mlp_group, attn_group]
        mark = grad
        while not all(group.done for group in groups):
            mark = advance([group for group in groups if not group.done], bits, mark)
        return [grad] + mlp_group.state + attn_group.state

    upper, grad, pairs_upper = backward(1, cotangent, saved[1])
    upper = lax.psum(upper, "dp")
    taken = (grad, saved[0], pairs_upper)
    grad, *arrived = lax.cond(
        lax.optimization_barrier(jnp.bool_(True)),
        lambda taken: backward(0, *taken),
        lambda taken: [
            jnp.zeros(item.shape, item.dtype)
            for item in jax.eval_shape(lambda taken: backward(0, *taken), taken)
        ],
        taken,
    )
    output = lax.reduce_precision(current, 8, 7).astype(bf16)
    output = (
        output.reshape(images, 2, 2, ROWS, D)[:, :, :, :WT]
        .reshape(images, 2, 2, WIN, WIN, D)
        .transpose(0, 1, 3, 2, 4, 5)
        .reshape(images, PIX, D)
    )
    pieces = [*arrived, upper]
    (
        qkv_g, proj_g, up_g, down_g, gains_g, shifts_g, qv_g, proj_b_g, up_b_g, down_b_g, heads,
    ) = pl.pallas_call(
        unpack_kernel,
        in_specs=[pl.BlockSpec(memory_space=pltpu.SMEM)]
        + [pl.BlockSpec(memory_space=pltpu.VMEM)] * len(pieces),
        out_specs=[pl.BlockSpec(memory_space=pltpu.VMEM)] * 11,
        out_shape=[
            shape(item.shape, f32)
            for item in (
                qkv_weight,
                proj_weight,
                fc1_weight,
                fc2_weight,
                norm_gains,
                norm_shifts,
                qv_bias,
                proj_bias,
                fc1_bias,
                fc2_bias,
            )
        ]
        + [shape((2, HEADS // 2, 256), f32)],
        scratch_shapes=[
            vmem((8, D // 2, D), bf16),
            vmem((8, D // 4 + 16, D), bf16),
            vmem((2, 32, D), f32),
        ],
        compiler_params=pltpu.CompilerParams(vmem_limit_bytes=30 * 1024 * 1024),
        name="unpack",
    )(bits, *pieces)
    table_g = heads[:, :, :RELS].transpose(0, 2, 1)
    return (
        output,
        grad,
        gains_g,
        shifts_g,
        qkv_g,
        qv_g,
        table_g,
        proj_g,
        proj_b_g,
        up_g,
        up_b_g,
        down_g,
        down_b_g,
    )


def solution(mesh):
    return jax.shard_map(
        body,
        mesh=mesh,
        in_specs=(
            P(("dp", "fsdp"), None, None),
            P(),
            P(),
            P(None, None, "fsdp"),
            P(None, None, "fsdp"),
            P(None, "fsdp", None),
            P(None, None, "fsdp"),
            P(None, None, "fsdp"),
            P(None, "fsdp", None),
            P(None, "fsdp"),
            P(None, "fsdp", None),
            P(None, "fsdp"),
            P(None, "fsdp", None),
            P(None, "fsdp"),
            P(("dp", "fsdp"), None, None),
        ),
        out_specs=(
            P(("dp", "fsdp"), None, None),
            P(("dp", "fsdp"), None, None),
            P(None, None, "fsdp"),
            P(None, None, "fsdp"),
            P(None, "fsdp", None),
            P(None, None, "fsdp"),
            P(None, None, "fsdp"),
            P(None, "fsdp", None),
            P(None, "fsdp"),
            P(None, "fsdp", None),
            P(None, "fsdp"),
            P(None, "fsdp", None),
            P(None, "fsdp"),
        ),
        check_vma=False,
    )
```

```python
import functools

import numpy as np

import jax
import jax.numpy as jnp
from jax import lax
from jax.experimental import pallas as pl
from jax.experimental.pallas import tpu as pltpu
from jax.sharding import PartitionSpec as P

D = 512
HEADS = 16
HD = 32
FF = 2048
WIN = 7
IMG = 14
SHIFT = 3
PIX = 196
WT = 49
RELS = 169
ROWS = 64
CELL = 256
QUADS = 4
TIE = 0
LIVE = 176

norm_eps = 1e-05
scale = HD**-0.5
f32 = jnp.float32
bf16 = jnp.bfloat16


def place(offset):
    rows = np.full((CELL,), -1, np.int64)
    for i in range(IMG):
        for j in range(IMG):
            window = (i // WIN) * 2 + j // WIN
            row = window * ROWS + (i % WIN) * WIN + j % WIN
            rows[row] = ((i + offset) % IMG) * IMG + (j + offset) % IMG
    return rows


def permutations():
    base, moved = place(0), place(SHIFT)
    lay = np.zeros((CELL, PIX), np.float32)
    lay[base >= 0, base[base >= 0]] = 1
    shifted = np.zeros((CELL, PIX), np.float32)
    shifted[moved >= 0, moved[moved >= 0]] = 1
    return lay, lay.T.copy(), shifted @ lay.T, lay @ shifted.T


def dot(a, b):
    return jnp.dot(a, b, preferred_element_type=f32)


def dot_nt(a, b):
    return lax.dot_general(a, b, (((1,), (1,)), ((), ())), preferred_element_type=f32)


def dot_tn(a, b):
    return lax.dot_general(a, b, (((0,), (0,)), ((), ())), preferred_element_type=f32)


def loop(count, step):
    def run(at, carry):
        step(at)
        return carry

    lax.fori_loop(0, count, run, 0)


def span(at, size):
    return pl.ds(pl.multiple_of(at * size, size), size)


def normal(values):
    centred = values - jnp.mean(values, -1, keepdims=True)
    spread = lax.rsqrt(jnp.mean(centred * centred, -1, keepdims=True) + norm_eps)
    return centred * spread, spread


def norm_rows(source, target, gain, shift, rows):
    def step(at):
        part = span(at, 128)
        unit, _ = normal(source[part, :])
        target[part, :] = (unit * gain + shift).astype(bf16)

    loop(rows // 128, step)


def norm_back(grad, source, gain, extra, target, rows):
    def step(at, sums):
        part = span(at, 128)
        dh = grad[part, :]
        unit, spread = normal(source[part, :])
        du = dh * gain
        back = spread * (
            du
            - jnp.mean(du, -1, keepdims=True)
            - unit * jnp.mean(du * unit, -1, keepdims=True)
        )
        target[part, :] = extra[part, :] + back
        return (
            sums[0] + jnp.sum(dh * unit, 0, keepdims=True),
            sums[1] + jnp.sum(dh, 0, keepdims=True),
        )

    zero = jnp.zeros((1, D), f32)
    return lax.fori_loop(0, rows // 128, step, (zero, zero))


def move(matrix, source, target, rows, columns):
    for image in range(rows // CELL):
        for at in range(columns // D):
            target[image * CELL : (image + 1) * CELL, at * D : (at + 1) * D] = dot(
                matrix, source[image * CELL : (image + 1) * CELL, at * D : (at + 1) * D]
            ).astype(bf16)


def fetch(core, layer, own, other, target, sems):
    half = own.shape[1]
    mine = pltpu.make_async_copy(
        own.at[layer], target.at[pl.ds(pl.multiple_of(core * half, half), half), :], sems.at[0]
    )
    theirs = pltpu.make_async_copy(
        other.at[layer],
        target.at[pl.ds(pl.multiple_of((1 - core) * half, half), half), :],
        sems.at[1],
    )
    mine.start()
    theirs.start()

    def wait():
        mine.wait()
        theirs.wait()

    return wait


def give(core, grads, keep, send, sems):
    one = pltpu.make_async_copy(grads.at[core], keep, sems.at[0])
    two = pltpu.make_async_copy(grads.at[1 - core], send, sems.at[1])
    one.start()
    two.start()
    one.wait()
    two.wait()


def head_masks():
    lanes = lax.broadcasted_iota(jnp.int32, (ROWS, 128), 1) // HD
    return [lanes == at for at in range(QUADS)]


def stack_heads(value, masks):
    zero = jnp.zeros_like(value)
    return jnp.concatenate([jnp.where(mask, value, zero) for mask in masks], axis=0)


def pick_heads(value, masks):
    result = value[:ROWS]
    for at in range(1, QUADS):
        result = jnp.where(masks[at], value[at * ROWS : (at + 1) * ROWS], result)
    return result


def attention_forward_kernel(
    layer,
    rows,
    core_ref,
    source,
    lay,
    to_moved,
    from_moved,
    small,
    bias,
    mask,
    qkv_own,
    qkv_other,
    proj_own,
    proj_other,
    middle,
    normed,
    qkv,
    probs,
    mixed,
    qkv_w,
    proj_w,
    tokens_in,
    work,
    sems,
):
    core = core_ref[0]
    wait_qkv = fetch(core, layer, qkv_own, qkv_other, qkv_w, sems.at[0])
    wait_proj = fetch(core, layer, proj_own, proj_other, proj_w, sems.at[1])
    if layer == 0:
        for image in range(rows // CELL):
            tokens_in[image * CELL : (image + 1) * CELL, :] = dot(lay[...], source[image])
    else:
        tokens_in = source
    norm_rows(tokens_in, normed, small[0:1, :], small[2:3, :], rows)
    if layer == 0:
        moved = normed
    else:
        move(to_moved[...], normed, work, rows, D)
        moved = work
    wait_qkv()
    for at in range(3):
        part = dot(moved[...], qkv_w[:, at * D : (at + 1) * D])
        if at == 0:
            part = part + small[4:5, :]
        if at == 2:
            part = part + small[5:6, :]
        qkv[:, at * D : (at + 1) * D] = part.astype(bf16)
    masks = head_masks()
    out = mixed if layer == 0 else work

    def window(at):
        part = span(at, ROWS)
        for quad in range(QUADS):
            lanes = slice(quad * 128, (quad + 1) * 128)
            queries = stack_heads(qkv[part, lanes], masks)
            keys = qkv[part, D + quad * 128 : D + (quad + 1) * 128]
            values = qkv[part, 2 * D + quad * 128 : 2 * D + (quad + 1) * 128]
            scores = scale * dot_nt(keys, queries) + bias[layer, quad]
            if layer:
                scores = scores + mask[at % 4]
            expo = jnp.exp(scores - jnp.max(scores, 0, keepdims=True))
            prob = expo / jnp.sum(expo, 0, keepdims=True)
            probs[at, quad] = prob
            mix = dot_tn(prob.astype(bf16), values)
            out[part, lanes] = pick_heads(mix, masks).astype(bf16)

    loop(rows // ROWS, window)
    if layer:
        move(from_moved[...], work, mixed, rows, D)
    wait_proj()
    middle[...] = tokens_in[...] + dot(mixed[...], proj_w[...]) + small[6:7, :]


def mlp_forward_kernel(
    layer,
    rows,
    core_ref,
    middle,
    small,
    up_own,
    up_other,
    down_own,
    down_other,
    result,
    normed,
    hidden,
    slope,
    up_w,
    down_w,
    sems,
):
    core = core_ref[0]
    wait_up = fetch(core, layer, up_own, up_other, up_w, sems.at[0])
    wait_down = fetch(core, layer, down_own, down_other, down_w, sems.at[1])
    norm_rows(middle, normed, small[1:2, :], small[3:4, :], rows)
    wait_up()

    def step(at):
        part = span(at, 256)
        inner = dot(normed[...], up_w[:, part])
        row = 8 + at // 2
        inner = inner + small[pl.ds(row, 1), span(at % 2, 256)]
        below = 0.5 * (1.0 + lax.erf(inner * (0.5**0.5)))
        hidden[:, part] = (inner * below).astype(bf16)
        slope[:, part] = (
            below + inner * (jnp.exp(-0.5 * inner * inner) * ((2 * np.pi) ** -0.5))
        ).astype(bf16)

    loop(FF // 256, step)
    wait_down()
    result[...] = (
        middle[...] + dot(hidden[...], down_w[...]) + small[7:8, :]
    ).astype(result.dtype)


def mlp_backward_kernel(
    layer,
    rows,
    core_ref,
    grad,
    lay,
    middle,
    normed,
    hidden,
    slope,
    small,
    up_own,
    up_other,
    down_own,
    down_other,
    middle_grad,
    sums,
    keep,
    send,
    up_w,
    down_w,
    grads,
    inner_grad,
    grad_in,
    low,
    turned,
    normed_grad,
    sems,
):
    core = core_ref[0]
    wait_up = fetch(core, layer, up_own, up_other, up_w, sems.at[0])
    wait_down = fetch(core, layer, down_own, down_other, down_w, sems.at[1])
    if layer == 1:
        for image in range(rows // CELL):
            grad_in[image * CELL : (image + 1) * CELL, :] = dot(lay[...], grad[image])
    else:
        grad_in = grad
    low[...] = grad_in[...].astype(bf16)
    sums[...] = jnp.zeros(sums.shape, f32)
    sums[2:3, :] = jnp.sum(low[...].astype(f32), 0, keepdims=True)
    turned[...] = normed[...].T
    wait_down()

    def step(at):
        part = span(at, 256)
        back = dot_nt(low[...], down_w[part, :]) * slope[:, part].astype(f32)
        back = back.astype(bf16)
        inner_grad[:, part] = back
        sums[pl.ds(3 + at // 2, 1), span(at % 2, 256)] = jnp.sum(
            back.astype(f32), 0, keepdims=True
        )
        down_grad = dot(hidden[:, part].T, low[...]).astype(bf16)
        grads[at // 4, pl.ds(pl.multiple_of(1024 + (at % 4) * 256, 256), 256), :] = down_grad
        up_grad = dot(turned[...], back).astype(bf16)
        place_at = pl.ds(pl.multiple_of((at // 2) * 256, 256), 256)
        lanes = span(at % 2, 256)
        grads[0, place_at, lanes] = up_grad[:256]
        grads[1, place_at, lanes] = up_grad[256:]

    loop(FF // 256, step)
    wait_up()
    normed_grad[...] = dot_nt(inner_grad[...], up_w[...])
    gain_sum, shift_sum = norm_back(normed_grad, middle, small[1:2, :], grad_in, middle_grad, rows)
    sums[0:1, :] = gain_sum
    sums[1:2, :] = shift_sum
    give(core, grads, keep, send, sems.at[2])


def attention_backward_kernel(
    layer,
    rows,
    core_ref,
    middle_grad,
    source,
    lay,
    unlay,
    to_moved,
    from_moved,
    normed,
    qkv,
    probs,
    mixed,
    small,
    qkv_own,
    qkv_other,
    proj_own,
    proj_other,
    source_grad,
    sums,
    pairs,
    keep,
    send,
    qkv_w,
    proj_w,
    grads,
    tokens_in,
    low,
    mix_grad,
    joined,
    moved_grad,
    turned,
    normed_grad,
    sems,
):
    core = core_ref[0]
    wait_qkv = fetch(core, layer, qkv_own, qkv_other, qkv_w, sems.at[0])
    wait_proj = fetch(core, layer, proj_own, proj_other, proj_w, sems.at[1])
    if layer == 0:
        for image in range(rows // CELL):
            tokens_in[image * CELL : (image + 1) * CELL, :] = dot(lay[...], source[image])
    else:
        tokens_in = source
    low[...] = middle_grad[...].astype(bf16)
    sums[...] = jnp.zeros(sums.shape, f32)
    sums[4:5, :] = jnp.sum(low[...].astype(f32), 0, keepdims=True)
    turned[...] = mixed[...].T
    for side in range(2):
        grads[side, 768:1024, :] = dot(turned[side * 256 : (side + 1) * 256, :], low[...]).astype(
            bf16
        )
    wait_proj()
    if layer == 0:
        mix_grad[...] = dot_nt(low[...], proj_w[...]).astype(bf16)
        target = joined
    else:
        moved_grad[:, :D] = dot_nt(low[...], proj_w[...]).astype(bf16)
        move(to_moved[...], moved_grad, mix_grad, rows, D)
        target = moved_grad
    pairs[...] = jnp.zeros(pairs.shape, f32)
    masks = head_masks()

    def window(at):
        part = span(at, ROWS)
        for quad in range(QUADS):
            queries = stack_heads(qkv[part, quad * 128 : (quad + 1) * 128], masks)
            keys = qkv[part, D + quad * 128 : D + (quad + 1) * 128]
            values = qkv[part, 2 * D + quad * 128 : 2 * D + (quad + 1) * 128]
            given = stack_heads(mix_grad[part, quad * 128 : (quad + 1) * 128], masks)
            prob = probs[at, quad]
            prob_grad = dot_nt(values, given)
            delta = jnp.sum(prob_grad * prob, 0, keepdims=True)
            score_grad = (prob * (prob_grad - delta)).astype(bf16)
            pairs[quad] += score_grad.astype(f32)
            values_grad = dot(prob.astype(bf16), given)
            keys_grad = scale * dot(score_grad, queries)
            queries_grad = scale * pick_heads(dot_tn(score_grad, keys), masks)
            target[part, quad * 128 : (quad + 1) * 128] = queries_grad.astype(bf16)
            target[part, D + quad * 128 : D + (quad + 1) * 128] = keys_grad.astype(bf16)
            target[part, 2 * D + quad * 128 : 2 * D + (quad + 1) * 128] = values_grad.astype(bf16)

    loop(rows // ROWS, window)
    if layer:
        move(from_moved[...], moved_grad, joined, rows, 3 * D)
    sums[2:3, :] = jnp.sum(joined[:, :D].astype(f32), 0, keepdims=True)
    sums[3:4, :] = jnp.sum(joined[:, 2 * D :].astype(f32), 0, keepdims=True)
    turned[...] = normed[...].T
    for at in range(3):
        for side in range(2):
            grads[side, at * 256 : (at + 1) * 256, :] = dot(
                turned[side * 256 : (side + 1) * 256, :], joined[:, at * D : (at + 1) * D]
            ).astype(bf16)
    wait_qkv()
    normed_grad[...] = dot_nt(joined[...], qkv_w[...])
    if layer == 0:
        gain_sum, shift_sum = norm_back(
            normed_grad, tokens_in, small[0:1, :], middle_grad, normed_grad, rows
        )
        for image in range(rows // CELL):
            value = normed_grad[image * CELL : (image + 1) * CELL, :]
            high = value.astype(bf16)
            rest = value - high.astype(f32)
            fine = rest.astype(bf16)
            last = (rest - fine.astype(f32)).astype(bf16)
            source_grad[image] = (
                dot(unlay[...], high) + dot(unlay[...], fine) + dot(unlay[...], last)
            )
    else:
        gain_sum, shift_sum = norm_back(
            normed_grad, tokens_in, small[0:1, :], middle_grad, source_grad, rows
        )
    sums[0:1, :] = gain_sum
    sums[1:2, :] = shift_sum
    give(core, grads, keep, send, sems.at[2])


def call(kernel, layer, rows, core, inputs, kinds, outs, out_kinds, scratch, flops):
    spaces = {"v": pltpu.VMEM, "a": pl.ANY}
    return pl.pallas_call(
        functools.partial(kernel, layer, rows),
        in_specs=[pl.BlockSpec(memory_space=pltpu.SMEM)]
        + [pl.BlockSpec(memory_space=spaces[kind]) for kind in kinds],
        out_specs=[pl.BlockSpec(memory_space=spaces[kind]) for kind in out_kinds],
        out_shape=outs,
        scratch_shapes=scratch,
        compiler_params=pltpu.CompilerParams(vmem_limit_bytes=30 * 1024 * 1024),
        cost_estimate=pl.CostEstimate(flops=1, bytes_accessed=1, transcendentals=0),
        name=kernel.__name__ + str(layer),
    )(core, *inputs)


def shape(dims, dtype):
    return jax.ShapeDtypeStruct(dims, dtype)


def swap_cores(value):
    return lax.ppermute(value, "fsdp", [(0, 1), (1, 0)])


def in_order(own, other, axis):
    first = lax.axis_index("fsdp") == 0
    return jnp.concatenate([jnp.where(first, own, other), jnp.where(first, other, own)], axis=axis)


def dp_swap(value, bit, count):
    return lax.ppermute(value, "dp", [(at, at ^ (1 << bit)) for at in range(count)])


def plus(one, two):
    return (one.astype(f32) + two.astype(f32)).astype(bf16)


def op_first(bits, ins, outs):
    quarter = outs[0].shape[0] // 2
    for part in range(2):
        keep, got = ins[2 * part : 2 * part + 2]
        send, hold = outs[2 * part : 2 * part + 2]
        side = bits[part]
        for low in range(2):
            rows = slice(low * quarter, (low + 1) * quarter)
            send[rows, :] = plus(keep[2 * (1 - side) + low], got[2 * (1 - side) + low])
            hold[rows, :] = plus(keep[2 * side + low], got[2 * side + low])


def op_first_small(bits, ins, outs):
    quarter = outs[0].shape[0] // 2
    rows_in = quarter - 16
    tiny, tiny_got = ins[4:6]
    for part in range(2):
        keep, got = ins[2 * part : 2 * part + 2]
        send, hold = outs[2 * part : 2 * part + 2]
        side = bits[part]
        for low in range(2):
            first = slice(low * quarter, low * quarter + rows_in)
            last = slice(low * quarter + rows_in, (low + 1) * quarter)
            for target, at in ((send, 2 * (1 - side) + low), (hold, 2 * side + low)):
                target[first, :] = plus(keep[at], got[at])
                target[last, :] = plus(tiny[4 * part + at], tiny_got[4 * part + at])


def op_second(bits, ins, outs):
    for part in range(2):
        hold, got = ins[2 * part : 2 * part + 2]
        send, rest = outs[2 * part : 2 * part + 2]
        side = bits[1 - part]
        send[...] = plus(hold[1 - side], got[1 - side])
        rest[...] = plus(hold[side], got[side])


def op_join(bits, ins, outs):
    quarter = ins[0].shape[0]
    for part in range(2):
        outs[0][part * quarter : (part + 1) * quarter, :] = plus(
            ins[2 * part][...], ins[2 * part + 1][...]
        )


def op_add(bits, ins, outs):
    outs[0][...] = plus(ins[0][...], ins[1][...])


def step_kernel(plan, bits_ref, *refs):
    bits = (bits_ref[0], bits_ref[1])
    total = sum(item[1] for item in plan)
    ins, outs = refs[:total], refs[total:]
    for op, inputs, outputs in plan:
        op(bits, ins[:inputs], outs[:outputs])
        ins, outs = ins[inputs:], outs[outputs:]


class Group:
    def __init__(self, rows, parts, count, tiny=None):
        self.small = tiny
        self.quarter = rows // 4 + (16 if tiny else 0)
        self.parts = parts
        self.count = count
        self.stage = 0
        self.later = count.bit_length() - 3
        self.done = False

    def low(self, rows):
        return shape((rows, D), bf16)

    def next_op(self):
        q = self.quarter
        if self.stage == 0:
            ins = [item.reshape(4, -1, D) for pair in self.parts for item in pair]
            if self.small:
                ins += [item.reshape(8, 16, D) for item in self.small]
            return op_first_small if self.small else op_first, ins, [self.low(2 * q)] * 4
        if self.stage == 1:
            ins = [item.reshape(2, q, D) for item in self.state]
            return op_second, ins, [self.low(q)] * 4
        if self.stage == 2:
            return op_join, self.state, [self.low(2 * q)]
        if self.stage < 3 + self.later:
            return op_add, self.state, [self.low(2 * q)]
        return None

    def send(self, outs):
        if self.stage < 2:
            first, second = (0, 1) if self.stage == 0 else (1, 0)
            self.state = [
                outs[1],
                dp_swap(outs[0], first, self.count),
                outs[3],
                dp_swap(outs[2], second, self.count),
            ]
        elif self.stage < 2 + self.later:
            self.state = [outs[0], dp_swap(outs[0], self.stage, self.count)]
        elif self.stage == 2 + self.later:
            mine = outs[0]
            self.state = [mine, dp_swap(mine, 0, self.count), dp_swap(mine, 1, self.count)]
        else:
            q = self.quarter
            mine, by_x, by_y = self.state
            self.state = [
                mine,
                by_x,
                by_y,
                dp_swap(by_x[:q], 1, self.count),
                dp_swap(by_y[q:], 0, self.count),
            ]
            self.done = True
        self.stage += 1


def after(first, then):
    return lax.optimization_barrier((first, then))[1]


def advance(groups, bits, when, final=False):
    ops, marks = [], []
    for group in groups:
        op = group.next_op()
        if op is None:
            group.state = list(after(when, group.state))
            group.send(None)
        else:
            ops.append((group, op))
    if not ops:
        return when
    plan = tuple((op[0], len(op[1]), len(op[2])) for _, op in ops)
    inputs = [item for _, op in ops for item in op[1]]
    outs = [item for _, op in ops for item in op[2]]
    inputs = after(when, inputs)
    results = pl.pallas_call(
        functools.partial(step_kernel, plan),
        in_specs=[pl.BlockSpec(memory_space=pltpu.SMEM)]
        + [pl.BlockSpec(memory_space=pltpu.VMEM)] * len(inputs),
        out_specs=[pl.BlockSpec(memory_space=pltpu.VMEM)] * len(outs),
        out_shape=outs,
        compiler_params=pltpu.CompilerParams(vmem_limit_bytes=30 * 1024 * 1024),
        cost_estimate=pl.CostEstimate(flops=1, bytes_accessed=1, transcendentals=0),
        name="reduce_step",
    )(bits, *inputs)
    for group, op in ops:
        mine, results = results[: len(op[2])], results[len(op[2]) :]
        group.send(mine)
        marks.append(mine[0])
    return marks[0]


def merge_kernel(*refs):
    out = refs[-1]
    start = 0
    for at in range(0, len(refs) - 1, 2):
        rows = refs[at].shape[0]
        out[start : start + rows, :] = plus(refs[at][...], refs[at + 1][...])
        start += rows


def quarters(ins, x, y, target):
    mine, by_x, by_y, far_first, far_second = ins
    q = far_first.shape[0]
    target[x * 2 + y] = mine[:q, :]
    target[(1 - x) * 2 + y] = by_x[:q, :]
    target[x * 2 + 1 - y] = by_y[:q, :]
    target[(1 - x) * 2 + 1 - y] = far_first[...]
    target[4 + y * 2 + x] = mine[q:, :]
    target[4 + y * 2 + 1 - x] = by_x[q:, :]
    target[4 + (1 - y) * 2 + x] = by_y[q:, :]
    target[4 + (1 - y) * 2 + 1 - x] = far_second[...]


def unpack_kernel(bits_ref, *refs):
    x, y, core = bits_ref[0], bits_ref[1], bits_ref[2]
    mlp_in, attn_in, upper = refs[:5], refs[5:10], refs[10]
    qkv_out, proj_out, up_out, down_out = refs[11:15]
    gains_out, shifts_out, qv_out, proj_b_out, up_b_out, down_b_out, table_out = refs[15:22]
    mlp, attn, tiny = refs[22:]
    half = D // 2
    for at in range(2):
        up_out[1, :, 2 * at * D : (2 * at + 1) * D] = upper[2 * at * half : (2 * at + 1) * half, :].astype(f32)
        up_out[1, :, (2 * at + 1) * D : (2 * at + 2) * D] = upper[
            (2 * at + 1) * half : (2 * at + 2) * half, :
        ].astype(f32)
    down_out[1] = upper[2 * D : 4 * D, :].astype(f32)
    for at in range(3):
        qkv_out[1, :, at * D : (at + 1) * D] = upper[
            4 * D + at * half : 4 * D + (at + 1) * half, :
        ].astype(f32)
    proj_out[1] = upper[4 * D + 3 * half : 6 * D, :].astype(f32)
    tiny[1, :16, :] = upper[6 * D :, :].astype(f32)
    quarters(mlp_in, x, y, mlp)
    quarters(attn_in, x, y, attn)
    for at in range(4):
        up_out[0, :, at * D : (at + 1) * D] = mlp[at].astype(f32)
        down_out[0, at * half : (at + 1) * half, :] = mlp[4 + at].astype(f32)
    q = half // 2
    for at in range(8):
        rows = slice((at % 2) * q, (at % 2 + 1) * q)
        value = attn[at, :q, :].astype(f32)
        if at < 6:
            qkv_out[0, rows, (at // 2) * D : (at // 2 + 1) * D] = value
        else:
            proj_out[0, rows, :] = value
    for at in range(2):
        tiny[0, at * 16 : (at + 1) * 16, :] = attn[at, q : q + 16, :].astype(f32)
    tiny[1, 16:, :] = attn[2, q : q + 16, :].astype(f32)
    first = core == 0

    def own(row):
        return jnp.where(first, row[:, :half], row[:, half:])

    for layer in range(2):
        sums = tiny[layer]
        for norm in range(2):
            gains_out[layer, norm : norm + 1, :] = own(sums[8 * norm : 8 * norm + 1])
            shifts_out[layer, norm : norm + 1, :] = own(sums[8 * norm + 1 : 8 * norm + 2])
            qv_out[layer, norm : norm + 1, :] = own(sums[2 + norm : 3 + norm])
            up_b_out[layer : layer + 1, norm * D : (norm + 1) * D] = jnp.where(
                first, sums[11 + norm : 12 + norm], sums[13 + norm : 14 + norm]
            )
        proj_b_out[layer : layer + 1, :] = own(sums[4:5])
        down_b_out[layer : layer + 1, :] = own(sums[10:11])
        table_out[layer] = jnp.where(first, sums[16:24, :256], sums[24:32, :256])


def body(
    tokens,
    regions,
    rel_index,
    norm_gains,
    norm_shifts,
    qkv_weight,
    qv_bias,
    rel_table,
    proj_weight,
    proj_bias,
    fc1_weight,
    fc1_bias,
    fc2_weight,
    fc2_bias,
    cotangent,
):
    count = lax.axis_size("dp")
    images = tokens.shape[0]
    rows = images * CELL
    windows = images * 4
    own_small = jnp.concatenate(
        [
            norm_gains,
            norm_shifts,
            qv_bias,
            proj_bias[:, None],
            fc2_bias[:, None],
            fc1_bias.reshape(2, 4, D // 2),
        ],
        axis=1,
    )
    own_table = rel_table
    qkv_other = swap_cores(qkv_weight)
    proj_other = swap_cores(proj_weight)
    other_small = swap_cores(own_small)
    other_table = swap_cores(own_table)
    up_other = swap_cores(fc1_weight)
    down_other = swap_cores(fc2_weight)

    core = lax.axis_index("fsdp").astype(jnp.int32).reshape(1)
    eight = in_order(own_small[:, :8], other_small[:, :8], 2)
    four = in_order(
        own_small[:, 8:].reshape(2, 2, D), other_small[:, 8:].reshape(2, 2, D), 1
    )
    small_all = jnp.concatenate([eight, four, jnp.zeros((2, 4, D), bf16)], axis=1).astype(f32)
    table = in_order(own_table, other_table, 2)
    table = jnp.concatenate(
        [table, jnp.full((2, 1, HEADS), -1e30, bf16), jnp.zeros((2, LIVE - RELS - 1, HEADS), bf16)],
        axis=1,
    )
    grid_index = rel_index.reshape(WT, WT).T
    grid_index = jnp.pad(grid_index, ((0, 0), (0, ROWS - WT)))
    grid_index = jnp.pad(grid_index, ((0, ROWS - WT), (0, 0)), constant_values=RELS)
    onehot = (
        grid_index.reshape(1, ROWS * ROWS) == jnp.arange(LIVE, dtype=jnp.int32)[:, None]
    ).astype(bf16)
    bias_all = jnp.einsum("lrh,rp->lhp", table, onehot, preferred_element_type=f32)
    bias_all = (
        bias_all.reshape(2, QUADS, 4, ROWS, ROWS)
        .transpose(0, 1, 3, 2, 4)
        .reshape(2, QUADS, ROWS, 4 * ROWS)
    )
    region_win = (
        regions.reshape(2, WIN, 2, WIN).transpose(0, 2, 1, 3).reshape(4, WT)
    )
    mask = jnp.where(region_win[:, :, None] == region_win[:, None, :], 0.0, -100.0).astype(f32)
    mask = jnp.pad(mask, ((0, 0), (0, ROWS - WT), (0, ROWS - WT)))
    mask = jnp.tile(mask, (1, 1, 4))
    lay, unlay, to_moved, from_moved = [jnp.asarray(item, bf16) for item in permutations()]

    vmem = pltpu.VMEM
    wide = (rows, D)
    attn_w = [vmem((D, 3 * D), bf16), vmem((D, D), bf16)]
    mlp_w = [vmem((D, FF), bf16), vmem((FF, D), bf16)]
    two_sems = pltpu.SemaphoreType.DMA((2, 2))
    three_sems = pltpu.SemaphoreType.DMA((3, 2))
    attn_flops = 2 * rows * D * D * 5
    mlp_flops = 2 * rows * D * FF * 2
    current = tokens
    saved = []
    for layer in range(2):
        small = small_all[layer]
        middle, normed, qkv, probs, mixed = call(
            attention_forward_kernel,
            layer,
            rows,
            core,
            [
                current,
                lay,
                to_moved,
                from_moved,
                small,
                bias_all,
                mask,
                qkv_weight,
                qkv_other,
                proj_weight,
                proj_other,
            ],
            "vvvvvvvaaaa",
            [
                shape(wide, f32),
                shape(wide, bf16),
                shape((rows, 3 * D), bf16),
                shape((windows, QUADS, ROWS, 4 * ROWS), f32),
                shape(wide, bf16),
            ],
            "vvvvv",
            attn_w + [vmem(wide if layer == 0 else (8, 128), f32), vmem(wide, bf16), two_sems],
            attn_flops,
        )
        result, normed_two, hidden, slope = call(
            mlp_forward_kernel,
            layer,
            rows,
            core,
            [middle, small, fc1_weight, up_other, fc2_weight, down_other],
            "vvaaaa",
            [
                shape(wide, f32),
                shape(wide, bf16),
                shape((rows, FF), bf16),
                shape((rows, FF), bf16),
            ],
            "vvvv",
            mlp_w + [two_sems],
            mlp_flops,
        )
        saved.append((current, middle, normed, qkv, probs, mixed, normed_two, hidden, slope, small))
        current = result
    at_dp = lax.axis_index("dp")
    bits = jnp.stack([at_dp & 1, (at_dp >> 1) & 1, lax.axis_index("fsdp")]).astype(jnp.int32)
    onehot_f = onehot.astype(f32)

    def table_rows(pairs):
        flat = (
            pairs.reshape(QUADS, ROWS, 4, ROWS).transpose(0, 2, 1, 3).reshape(HEADS, -1)
        )
        heads = jnp.einsum("hp,rp->hr", flat, onehot_f, precision=lax.Precision.HIGH)
        return jnp.pad(heads, ((0, 0), (0, D - LIVE)))

    def backward(layer, grad, kept, pairs_upper=None):
        source, middle, normed, qkv, probs, mixed, normed_two, hidden, slope, small = kept
        middle_grad, mlp_sums, mlp_keep, mlp_send = call(
            mlp_backward_kernel,
            layer,
            rows,
            core,
            [
                grad,
                lay,
                middle,
                normed_two,
                hidden,
                slope,
                small,
                fc1_weight,
                up_other,
                fc2_weight,
                down_other,
            ],
            "vvvvvvvaaaa",
            [
                shape(wide, f32),
                shape((8, D), f32),
                shape((FF, D), bf16),
                shape((FF, D), bf16),
            ],
            "vvaa",
            mlp_w
            + [
                vmem((2, FF, D), bf16),
                vmem((rows, FF), bf16),
                vmem(wide if layer == 1 else (8, 128), f32),
                vmem(wide, bf16),
                vmem((D, rows), bf16),
                vmem(wide, f32),
                three_sems,
            ],
            2 * mlp_flops,
        )
        mlp_got = swap_cores(mlp_send)
        if layer == 0:
            mlp_group = Group(2 * D, [
                (mlp_keep[: 2 * D], mlp_got[: 2 * D]),
                (mlp_keep[2 * D :], mlp_got[2 * D :]),
            ], count)
            mark = advance([mlp_group], bits, mlp_sums)
            middle_grad = after(mark, middle_grad)
        grad, attn_sums, pairs, attn_keep, attn_send = call(
            attention_backward_kernel,
            layer,
            rows,
            core,
            [
                middle_grad,
                source,
                lay,
                unlay,
                to_moved,
                from_moved,
                normed,
                qkv,
                probs,
                mixed,
                small,
                qkv_weight,
                qkv_other,
                proj_weight,
                proj_other,
            ],
            "vvvvvvvvvvvaaaa",
            [
                shape(wide if layer else (images, PIX, D), f32),
                shape((8, D), f32),
                shape((QUADS, ROWS, 4 * ROWS), f32),
                shape((2 * D, D), bf16),
                shape((2 * D, D), bf16),
            ],
            "vvvaa",
            attn_w
            + [
                vmem((2, 2 * D, D), bf16),
                vmem(wide if layer == 0 else (8, 128), f32),
                vmem(wide, bf16),
                vmem(wide, bf16),
                vmem((rows, 3 * D), bf16),
                vmem((rows, 3 * D) if layer else (16, 128), bf16),
                vmem((D, rows), bf16),
                vmem(wide, f32),
                three_sems,
            ],
            2 * attn_flops,
        )
        if layer == 0:
            held = (grad, attn_sums, pairs, attn_keep, attn_send, mlp_group.state)
            grad, attn_sums, pairs, attn_keep, attn_send, mlp_group.state = (
                lax.optimization_barrier(held)
            )
        attn_got = swap_cores(attn_send)
        tiny = [attn_sums, mlp_sums]
        if layer == 0:
            tiny += [table_rows(pairs), table_rows(pairs_upper)]
        tiny = jnp.concatenate(tiny, axis=0).astype(bf16)
        tiny_got = swap_cores(tiny)
        if layer == 1:
            upper = pl.pallas_call(
                merge_kernel,
                out_shape=shape((6 * D + 16, D), bf16),
                compiler_params=pltpu.CompilerParams(vmem_limit_bytes=30 * 1024 * 1024),
                name="merge",
            )(mlp_keep, mlp_got, attn_keep, attn_got, tiny, tiny_got)
            return lax.optimization_barrier((upper, grad, pairs))
        pad = ((0, 80), (0, 0))
        attn_group = Group(
            D,
            [(attn_keep[:D], attn_got[:D]), (attn_keep[D:], attn_got[D:])],
            count,
            (jnp.pad(tiny, pad), jnp.pad(tiny_got, pad)),
        )
        groups = [mlp_group, attn_group]
        mark = grad
        while not all(group.done for group in groups):
            mark = advance([group for group in groups if not group.done], bits, mark)
        return [grad] + mlp_group.state + attn_group.state

    upper, grad, pairs_upper = backward(1, cotangent, saved[1])
    upper = lax.psum(upper, "dp")
    taken = (grad, saved[0], pairs_upper)
    grad, *arrived = lax.cond(
        lax.optimization_barrier(jnp.bool_(True)),
        lambda taken: backward(0, *taken),
        lambda taken: [
            jnp.zeros(item.shape, item.dtype)
            for item in jax.eval_shape(lambda taken: backward(0, *taken), taken)
        ],
        taken,
    )
    output = lax.reduce_precision(current, 8, 7).astype(bf16)
    output = (
        output.reshape(images, 2, 2, ROWS, D)[:, :, :, :WT]
        .reshape(images, 2, 2, WIN, WIN, D)
        .transpose(0, 1, 3, 2, 4, 5)
        .reshape(images, PIX, D)
    )
    pieces = [*arrived, upper]
    (
        qkv_g, proj_g, up_g, down_g, gains_g, shifts_g, qv_g, proj_b_g, up_b_g, down_b_g, heads,
    ) = pl.pallas_call(
        unpack_kernel,
        in_specs=[pl.BlockSpec(memory_space=pltpu.SMEM)]
        + [pl.BlockSpec(memory_space=pltpu.VMEM)] * len(pieces),
        out_specs=[pl.BlockSpec(memory_space=pltpu.VMEM)] * 11,
        out_shape=[
            shape(item.shape, f32)
            for item in (
                qkv_weight,
                proj_weight,
                fc1_weight,
                fc2_weight,
                norm_gains,
                norm_shifts,
                qv_bias,
                proj_bias,
                fc1_bias,
                fc2_bias,
            )
        ]
        + [shape((2, HEADS // 2, 256), f32)],
        scratch_shapes=[
            vmem((8, D // 2, D), bf16),
            vmem((8, D // 4 + 16, D), bf16),
            vmem((2, 32, D), f32),
        ],
        compiler_params=pltpu.CompilerParams(vmem_limit_bytes=30 * 1024 * 1024),
        name="unpack",
    )(bits, *pieces)
    table_g = heads[:, :, :RELS].transpose(0, 2, 1)
    return (
        output,
        grad,
        gains_g,
        shifts_g,
        qkv_g,
        qv_g,
        table_g,
        proj_g,
        proj_b_g,
        up_g,
        up_b_g,
        down_g,
        down_b_g,
    )


def solution(mesh):
    return jax.shard_map(
        body,
        mesh=mesh,
        in_specs=(
            P(("dp", "fsdp"), None, None),
            P(),
            P(),
            P(None, None, "fsdp"),
            P(None, None, "fsdp"),
            P(None, "fsdp", None),
            P(None, None, "fsdp"),
            P(None, None, "fsdp"),
            P(None, "fsdp", None),
            P(None, "fsdp"),
            P(None, "fsdp", None),
            P(None, "fsdp"),
            P(None, "fsdp", None),
            P(None, "fsdp"),
            P(("dp", "fsdp"), None, None),
        ),
        out_specs=(
            P(("dp", "fsdp"), None, None),
            P(("dp", "fsdp"), None, None),
            P(None, None, "fsdp"),
            P(None, None, "fsdp"),
            P(None, "fsdp", None),
            P(None, None, "fsdp"),
            P(None, None, "fsdp"),
            P(None, "fsdp", None),
            P(None, "fsdp"),
            P(None, "fsdp", None),
            P(None, "fsdp"),
            P(None, "fsdp", None),
            P(None, "fsdp"),
        ),
        check_vma=False,
    )
```
